32 devices in a mesh: slab: 2 (over x), inline: 8 (over z, y), xline: 2 (over core).
Axes of the slice: x: 2, y: 2, z: 4, core: 2. Of those that a mesh axis runs over, the one named last changes fastest.
Arguments:
- traces: bfloat16 [256, 48, 128], P(('slab', 'inline'), 'xline'), parts along dimension 0, may hold values from -15 to 15
- directions: int32 [10], replicated, may hold values from 0 to 31
- init_means: float32 [32, 20], replicated, may hold values from 0.3 to 2.5
- init_variances: float32 [32, 20], replicated, may hold values from 0.01 to 0.2
- init_weights: float32 [32], replicated, may hold values from 0.01 to 1
Outputs:
- posterior: bfloat16 [256, 32, 48, 128], P(('slab', 'inline'), None, 'xline'), parts along dimension 0
- final_means: float32 [64, 20], P('slab'), parts along dimension 0
- final_variances: float32 [64, 20], P('slab'), parts along dimension 0
- final_weights: float32 [64], P('slab'), parts along dimension 0
The draws below stay inside these ranges and needn't reach their ends.
There are 2 independent parts, one for each index of `slab`. The reference program is written for one: setup_inputs(seed, part) draws one part's arguments, and reference() takes and returns one part's arrays. A program takes and returns all parts, laid end to end along the dimension named above; an argument that names none is the same for every part. Nothing has to cross between parts.
All inputs are finite; a program needn't handle non-finite values.
Results may differ from the reference program's by a relative error of at most 0.001.
The reference program's roundings to bfloat16 on the way count: a program that leaves them out, or rounds other values in their place, can miss the bound.
Values may be sent and summed in bfloat16 or wider, within the bound.
No kernel may reach another device: no remote copies, remote signals or barrier semaphores. Data moves between devices by JAX's collectives and lax.ppermute only.
A program may use at most 64 MiB of HBM per device.

```python
import math
import jax
import jax.numpy as jnp
import numpy as np
from jax import lax

NT = 128
ORIENTS = 10
FEATS = 20
K = 32
TAPS = 31
HALF = 15
AZIMUTHS = 8
DIPS = 4
ITERS = 2
NI = 128
NX = 48
CELLS = 786432


def draw_traces(key, part):
    position = jnp.arange(NI).astype(jnp.float32) / max(NI - 1, 1)
    drawn_values = jnp.clip(jax.random.normal(key, (NI, NX, NT), jnp.float32), -5.0, 5.0)
    amplitude = 3.0 ** position
    return jnp.clip(drawn_values * amplitude[:, None, None], -15.0, 15.0).astype(jnp.bfloat16)


def set_ends(values, key, smallest, high):
    shape = values.shape
    place = [jax.random.randint(jax.random.fold_in(key, axis), (), 0, shape[axis]) for axis in range(len(shape))]
    values = values.at[tuple(place)].set(smallest)
    longest = shape.index(max(shape))
    place[longest] = (place[longest] + 1) % shape[longest]
    return values.at[tuple(place)].set(high)


def setup_inputs(seed: int = 0, part: int = 0) -> dict:
    seeds = jax.random.split(jax.random.key(seed), 6)
    part_keys = jax.random.split(jax.random.fold_in(seeds[5], part), 6)
    return {
        "traces": draw_traces(jax.random.fold_in(jax.random.fold_in(seeds[5], part), 71), part),
        "directions": set_ends(jax.random.randint(seeds[1], (ORIENTS,), 0, AZIMUTHS * DIPS), jax.random.fold_in(seeds[1], 1), 0, (AZIMUTHS * DIPS) - 1).astype(jnp.int32),
        "init_means": jnp.clip(jax.random.uniform(seeds[2], (K, FEATS), jnp.float32, 0.3, 2.5), 0.3, 2.5),
        "init_variances": jnp.clip(jnp.exp(jax.random.uniform(seeds[3], (K, FEATS), jnp.float32, math.log(0.01), math.log(0.2))), 0.01, 0.2),
        "init_weights": jnp.clip(jnp.exp(jax.random.uniform(seeds[4], (K,), jnp.float32, math.log(0.01), math.log(1.0))), 0.01, 1.0),
    }


eps_mag = 0.01
wavenumber = math.pi / 4.0
highest = lax.Precision.HIGHEST
cross_real = np.array([[[1.0, 0.0], [1.0, 0.0]], [[0.0, 1.0], [0.0, -1.0]]], np.float32)
cross_imag = np.array([[[0.0, 1.0], [0.0, 1.0]], [[-1.0, 0.0], [1.0, 0.0]]], np.float32)

def tap_table(directions):
    azimuth = (directions % AZIMUTHS).astype(jnp.float32) * (math.pi / AZIMUTHS)
    dip_angle = (directions // AZIMUTHS + 1).astype(jnp.float32) * (math.pi / (2 * DIPS + 2))
    wave_vector = wavenumber * jnp.stack([jnp.sin(dip_angle) * jnp.cos(azimuth), jnp.sin(dip_angle) * jnp.sin(azimuth), jnp.cos(dip_angle)], axis=1)
    offsets = jnp.arange(TAPS).astype(jnp.float32) - HALF
    width_scale = HALF / 3.0
    envelope = jnp.exp(-offsets * offsets / (2.0 * width_scale * width_scale))
    envelope = envelope / jnp.sqrt(jnp.sum(envelope * envelope))
    phases = wave_vector[:, :, None] * offsets[None, None, :]
    return jnp.stack([envelope * jnp.cos(phases), envelope * jnp.sin(phases)], axis=2).astype(jnp.bfloat16)

def band_onehot(rows_in, rows_out, offset_base):
    difference = jnp.arange(rows_in).astype(jnp.int32)[:, None] - jnp.arange(rows_out).astype(jnp.int32)[None, :] + offset_base
    return (difference[:, :, None] == jnp.arange(TAPS).astype(jnp.int32)[None, None, :]).astype(jnp.float32)

def log_scores(feature_rows, centers, spreads, log_weights):
    inverse = 1.0 / spreads
    offset_term = log_weights - 0.5 * lax.optimization_barrier(jnp.sum(jnp.log(2.0 * math.pi * spreads), axis=1))
    distance = lax.optimization_barrier(jnp.sum((feature_rows[None, :, :] - centers[:, :, None]) ** 2 * inverse[:, :, None], axis=1))
    return offset_term[:, None] - 0.5 * distance

def posterior_weights(feature_rows, centers, spreads, log_weights):
    scores = log_scores(feature_rows, centers, spreads, log_weights)
    largest = lax.optimization_barrier(jnp.max(scores, axis=0, keepdims=True))
    exponent = jnp.exp(scores - largest)
    return exponent / lax.optimization_barrier(jnp.sum(exponent, axis=0, keepdims=True))

def first_pass(feature_rows, centers, spreads, log_weights):
    posterior = posterior_weights(feature_rows, centers, spreads, log_weights)
    return (posterior.astype(jnp.bfloat16), lax.optimization_barrier(jnp.sum(posterior, axis=1)), jnp.einsum('km,fm->kf', posterior, feature_rows, precision=highest))

def centred_pass(feature_rows, centers, spreads, log_weights, new_centers):
    posterior = posterior_weights(feature_rows, centers, spreads, log_weights)
    return lax.optimization_barrier(jnp.sum(posterior[:, None, :] * (feature_rows[None, :, :] - new_centers[:, :, None]) ** 2, axis=2))

def reference(traces, directions, init_means, init_variances, init_weights):
    tap_values = tap_table(directions)
    wide_taps = tap_values.astype(jnp.float32)
    time_mats = jnp.einsum('stn,orn->osrt', band_onehot(NT, NT, HALF), wide_taps[:, 2], precision=highest).astype(jnp.bfloat16)
    xline_taps = jnp.einsum('pqr,on->opqrn', cross_real, wide_taps[:, 1, 0]) + jnp.einsum('pqr,on->opqrn', cross_imag, wide_taps[:, 1, 1])
    xline_mats = jnp.einsum('xyn,opqrn->oxpqry', band_onehot(NX, NX, HALF), xline_taps, precision=highest).astype(jnp.bfloat16)
    inline_taps = tap_values[:, 0]
    flat_traces = traces.reshape(NI * NX, NT)

    def orient_features(pieces):
        time_one, xline_one, inline_one = pieces
        band = jnp.dot(flat_traces, time_one.reshape(NT, 2 * NT), preferred_element_type=jnp.float32)
        band = band.astype(jnp.bfloat16).reshape(NI, NX, 2, NT)
        across = jnp.einsum('ixpt,xpqry->iqryt', band.astype(jnp.float32), xline_one.astype(jnp.float32), precision=highest).astype(jnp.bfloat16)
        padded = jnp.pad(across.astype(jnp.float32), ((HALF, HALF), (0, 0), (0, 0), (0, 0), (0, 0)))
        real_part = jnp.zeros((NI, 2, NX, NT), jnp.float32)
        imag_part = jnp.zeros((NI, 2, NX, NT), jnp.float32)
        for shift_index in range(TAPS):
            window = padded[shift_index:shift_index + NI]
            tap_real = inline_one[0, shift_index].astype(jnp.float32)
            tap_imag = inline_one[1, shift_index].astype(jnp.float32)
            real_part = real_part + window[:, :, 0] * tap_real - window[:, :, 1] * tap_imag
            imag_part = imag_part + window[:, :, 0] * tap_imag + window[:, :, 1] * tap_real
        return jnp.sqrt(real_part * real_part + imag_part * imag_part + eps_mag)
    stacked = lax.map(orient_features, (time_mats, xline_mats, inline_taps))
    features = jnp.transpose(stacked, (1, 0, 2, 3, 4)).reshape(NI, FEATS, NX * NT)
    centers = init_means
    spreads = init_variances
    weights = init_weights
    log_weights = jnp.log(init_weights)
    posterior = None
    for iteration in range(ITERS):
        posterior, masses, firsts = lax.map(lambda feature_rows: first_pass(feature_rows, centers, spreads, log_weights), features)
        total_mass = lax.optimization_barrier(jnp.sum(masses, axis=0))
        total_first = lax.optimization_barrier(jnp.sum(firsts, axis=0))
        new_centers = (total_first + centers) / (total_mass + 1.0)[:, None]
        spread_rows = lax.map(lambda feature_rows: centred_pass(feature_rows, centers, spreads, log_weights, new_centers), features)
        new_spreads = (lax.optimization_barrier(jnp.sum(spread_rows, axis=0)) + spreads) / (total_mass + 1.0)[:, None]
        weights = (total_mass + 1.0) / (CELLS + K)
        log_weights = jnp.log(weights)
        centers = new_centers
        spreads = new_spreads
    return (posterior.reshape(NI, K, NX, NT), centers, spreads, weights)
```

```python
import functools
import math

import jax
import jax.numpy as jnp
from jax import lax
from jax.experimental import pallas as pl
from jax.experimental.pallas import tpu as pltpu
from jax.sharding import PartitionSpec as P

TAPS = 31
HALF = 15
AZIMUTHS = 8
DIPS = 4
LANES = 128
SUBLANES = 8

eps_mag = 0.01
wavenumber = math.pi / 4.0


def round_up(value, step):
    return (value + step - 1) // step * step


def tap_table(directions):
    azimuth = (directions % AZIMUTHS).astype(jnp.float32) * (math.pi / AZIMUTHS)
    dip_angle = (directions // AZIMUTHS + 1).astype(jnp.float32) * (math.pi / (2 * DIPS + 2))
    wave_vector = wavenumber * jnp.stack(
        [
            jnp.sin(dip_angle) * jnp.cos(azimuth),
            jnp.sin(dip_angle) * jnp.sin(azimuth),
            jnp.cos(dip_angle),
        ],
        axis=1,
    )
    offsets = jnp.arange(TAPS).astype(jnp.float32) - HALF
    width_scale = HALF / 3.0
    envelope = jnp.exp(-offsets * offsets / (2.0 * width_scale * width_scale))
    envelope = envelope / jnp.sqrt(jnp.sum(envelope * envelope))
    phases = wave_vector[:, :, None] * offsets[None, None, :]
    return jnp.stack([envelope * jnp.cos(phases), envelope * jnp.sin(phases)], axis=2).astype(
        jnp.bfloat16
    )


def split3(values):
    high = values.astype(jnp.bfloat16)
    rest = values - high.astype(jnp.float32)
    middle = rest.astype(jnp.bfloat16)
    low = (rest - middle.astype(jnp.float32)).astype(jnp.bfloat16)
    return high, middle, low


def matrices_kernel(dims, taps_ref, time_ref, xline_ref, inline_ref):
    orients, samples, cols, rows, window = dims
    side = lax.axis_index("xline")
    lanes = lax.broadcasted_iota(jnp.int32, (SUBLANES, LANES), 1)[:1]

    def sheared(line, count, shift, width):
        wide = jnp.broadcast_to(line[:, :width], (count, width))
        return pltpu.roll(wide, shift % width, 1, stride=1, stride_axis=0)

    for orient in range(orients):
        line = lambda axis, part: taps_ref[pl.ds(orient * 6 + axis * 2 + part, 1), :]
        for part in range(2):
            time_ref[orient, :, part * samples : (part + 1) * samples] = sheared(
                line(2, part), samples, 2 * samples - HALF, 2 * samples
            )[:, :samples].astype(jnp.bfloat16)

        def xline_half(part, half, slot):
            shift = LANES - HALF + slot * cols
            if half:
                moved = jnp.where(
                    side == 0,
                    sheared(line(1, part), cols, shift + LANES - cols, LANES),
                    sheared(line(1, part), cols, shift + cols, LANES),
                )
            else:
                moved = sheared(line(1, part), cols, shift, LANES)
            return jnp.where((lanes >= slot * cols) & (lanes < (slot + 1) * cols), moved, 0.0)

        cosine = [xline_half(0, 0, p * 2) + xline_half(0, 1, p * 2 + 1) for p in range(2)]
        sine = [xline_half(1, 0, p * 2) + xline_half(1, 1, p * 2 + 1) for p in range(2)]
        xline_ref[orient] = jnp.concatenate(
            [
                cosine[0] - sine[1],
                sine[0] + cosine[1],
                cosine[0] + sine[1],
                sine[0] - cosine[1],
            ],
            axis=0,
        )[:, : 4 * cols].astype(jnp.bfloat16)

        def inline_part(part, slot):
            moved = sheared(line(0, part), rows, slot * window, LANES)
            return jnp.where((lanes >= slot * window) & (lanes < (slot + 1) * window), moved, 0.0)

        inline_ref[orient] = jnp.concatenate(
            [
                inline_part(0, 0) - inline_part(1, 1),
                inline_part(1, 0) + inline_part(0, 1),
            ],
            axis=0,
        )[:, : 2 * window].astype(jnp.bfloat16)


def score_matrix(centers, spreads, log_weights, feats, slot):
    lanes = lax.broadcasted_iota(jnp.int32, centers.shape, 1)
    real = lanes < feats
    inverse = jnp.where(real, 1.0 / spreads, 0.0)
    linear = jnp.where(real, centers * inverse, 0.0)
    logs = jnp.where(real, jnp.log(2.0 * math.pi * spreads), 0.0)
    terms = logs + jnp.where(real, centers * linear, 0.0)
    constant = log_weights - 0.5 * jnp.sum(terms, axis=1, keepdims=True)
    packed = linear + jnp.where(lanes == feats, constant, 0.0)
    packed = packed + pltpu.roll(-0.5 * inverse, slot, 1)
    wide = jnp.concatenate([packed, jnp.zeros_like(packed)], axis=1)
    high, middle, low = [piece.astype(jnp.float32) for piece in split3(wide)]
    second = lambda piece: pltpu.roll(piece, 2 * slot, 1)
    third = lambda piece: pltpu.roll(piece, 4 * slot, 1)
    return jnp.concatenate(
        [high + second(high) + third(high), middle + second(middle), low], axis=0
    )[:, : 6 * slot].astype(jnp.bfloat16)


def column(line, count):
    row_ids = lax.broadcasted_iota(jnp.int32, (count, LANES), 0)
    lane_ids = lax.broadcasted_iota(jnp.int32, (count, LANES), 1)
    return jnp.sum(jnp.where(row_ids == lane_ids, line, 0.0), axis=1, keepdims=True)


def expectation(features, matrix, components):
    both = jnp.concatenate([features, features * features], axis=0)
    data = jnp.concatenate(split3(both), axis=0)
    scores = jnp.dot(matrix, data, preferred_element_type=jnp.float32)
    scores = (
        scores[:components]
        + scores[components : 2 * components]
        + scores[2 * components : 3 * components]
    )
    exponent = jnp.exp(scores - jnp.max(scores, axis=0, keepdims=True))
    shares = exponent * (1.0 / jnp.sum(exponent, axis=0, keepdims=True))
    high = shares.astype(jnp.bfloat16)
    low = (shares - high.astype(jnp.float32)).astype(jnp.bfloat16)
    sums = lax.dot_general(
        jnp.concatenate([high, low], axis=0),
        data,
        (((1,), (1,)), ((), ())),
        preferred_element_type=jnp.float32,
    )
    return shares, sums


def gathered(features_ref, first, count, slot):
    place = lambda k: pl.multiple_of((first + k) * slot, SUBLANES)
    return jnp.concatenate([features_ref[pl.ds(place(k), slot), :] for k in range(count)], axis=1)


def fold_sums(sums, components, slot):
    both = sums[:components] + sums[components:]
    wide = jnp.concatenate(
        [both, jnp.zeros((components, 2 * LANES - 6 * slot), jnp.float32)], axis=1
    )
    total = wide + pltpu.roll(wide, 2 * LANES - 2 * slot, 1) + pltpu.roll(
        wide, 2 * LANES - 4 * slot, 1
    )
    return total[:, :LANES]


def features_kernel(dims, *refs):
    orients, samples, cols, rows, window, components, chunk = dims
    halves, refs = refs[:6], refs[6:]
    time_ref, xline_ref, inline_ref, means_ref, variances_ref, weights_ref = refs[:6]
    features_ref, sums_ref, traces, across, params, total = refs[6:]
    feats = 2 * orients
    slot = round_up(feats + 1, SUBLANES)
    orient = pl.program_id(0)
    @pl.when(orient == 0)
    def _():
        own, other, swap_one, swap_one_other, swap_two, swap_two_other = halves
        even = lax.rem(lax.axis_index("inline"), 2) == 0

        def put(place, near, far):
            traces[pl.ds(place * 2 * cols, 2 * cols), :] = jnp.concatenate(
                [near.astype(jnp.float32), far.astype(jnp.float32)], axis=0
            ).astype(jnp.bfloat16)

        for row in range(rows):
            put(HALF + row, own[row], other[row])
            one = swap_one[row].astype(jnp.float32)
            one_far = swap_one_other[row].astype(jnp.float32)
            two = swap_two[row].astype(jnp.float32)
            two_far = swap_two_other[row].astype(jnp.float32)
            if row >= rows - HALF:
                put(row - (rows - HALF), jnp.where(even, two, one), jnp.where(even, two_far, one_far))
            if row < HALF:
                put(HALF + rows + row, jnp.where(even, one, two), jnp.where(even, one_far, two_far))
        for place in range(rows + 2 * HALF, window):
            traces[pl.ds(place * 2 * cols, 2 * cols), :] = jnp.zeros(
                (2 * cols, samples), jnp.bfloat16
            )
        blank = lax.broadcasted_iota(jnp.int32, (slot - feats, samples), 0) == 0

        @pl.loop(0, rows * cols)
        def _(cell):
            features_ref[pl.ds(cell * slot + feats, slot - feats), :] = blank.astype(jnp.float32)

    lines = 2 * cols
    for pair in range(window // 2):
        block = traces[pl.ds(pair * 2 * lines, 2 * lines), :]
        band = jnp.dot(block, time_ref[0], preferred_element_type=jnp.float32)
        stacked = jnp.concatenate(
            [
                jnp.concatenate(
                    [band[:lines, p * samples : (p + 1) * samples] for p in range(2)], axis=0
                ),
                jnp.concatenate(
                    [band[lines:, p * samples : (p + 1) * samples] for p in range(2)], axis=0
                ),
            ],
            axis=1,
        ).astype(jnp.bfloat16)
        crossed = jnp.dot(xline_ref[0], stacked, preferred_element_type=jnp.float32)
        for k in range(2):
            across[pl.ds(2 * pair + k, 4 * cols, stride=window), :] = crossed[
                :, k * samples : (k + 1) * samples
            ]
    for polarity in range(2):
        for col in range(0, cols, 2):

            def taken(k, part):
                place = ((polarity * 2 + part) * cols + col + k) * window
                return across[pl.ds(place, window), :]

            stacked = jnp.concatenate(
                [jnp.concatenate([taken(k, 0), taken(k, 1)], axis=0) for k in range(2)], axis=1
            ).astype(jnp.bfloat16)
            found = jnp.dot(inline_ref[0], stacked, preferred_element_type=jnp.float32)
            real_part, imag_part = found[:rows], found[rows:]
            size = jnp.sqrt(real_part * real_part + imag_part * imag_part + eps_mag)
            for k in range(2):
                place = (col + k) * slot + 2 * orient + polarity
                features_ref[pl.ds(place, rows, stride=cols * slot), :] = size[
                    :, k * samples : (k + 1) * samples
                ]

    @pl.when(orient == orients - 1)
    def _():
        params[...] = jnp.ones(params.shape, jnp.float32)
        params[:components, :feats] = means_ref[...]
        params[components:, :feats] = variances_ref[...]
        log_weights = jnp.log(column(jnp.concatenate(
            [weights_ref[...], jnp.ones((1, LANES - components), jnp.float32)], axis=1), components))
        matrix = score_matrix(params[:components], params[components:], log_weights, feats, slot)
        total[...] = jnp.zeros(total.shape, jnp.float32)

        @pl.loop(0, rows)
        def _(row):
            partial = jnp.zeros(total.shape, jnp.float32)
            for start in range(0, cols, chunk):
                block = gathered(features_ref, row * cols + start, chunk, slot)
                partial = partial + expectation(block, matrix, components)[1]
            total[...] += partial

        sums_ref[...] = fold_sums(total[...], components, slot)


def new_params(sums, centers, spreads, feats, slot, cells):
    components = centers.shape[0]
    mass = sums[:, feats : feats + 1]
    first = sums
    second = pltpu.roll(sums, LANES - slot, 1)
    scale = 1.0 / (mass + 1.0)
    moved = (first + centers) * scale
    centred = second - 2.0 * moved * first + moved * moved * mass
    return moved, (centred + spreads) * scale, (mass + 1.0) / (cells + components)


def posterior_kernel(dims, *refs):
    orients, samples, cols, rows, components, chunk, cells = dims
    features_ref, means_ref, variances_ref, before_ref = refs[:4]
    posterior_ref, sums_ref, centers_ref, spreads_ref, matrix, total, turned = refs[4:]
    feats = 2 * orients
    slot = round_up(feats + 1, SUBLANES)
    row = pl.program_id(0)
    @pl.when(row == 0)
    def _():
        centers_ref[...] = jnp.zeros(centers_ref.shape, jnp.float32)
        spreads_ref[...] = jnp.ones(spreads_ref.shape, jnp.float32)
        centers_ref[:, :feats] = means_ref[...]
        spreads_ref[:, :feats] = variances_ref[...]
        centers, spreads, weights = new_params(
            before_ref[...], centers_ref[...], spreads_ref[...], feats, slot, cells
        )
        lanes = lax.broadcasted_iota(jnp.int32, centers.shape, 1)
        centers = jnp.where(lanes < feats, centers, 0.0)
        spreads = jnp.where(lanes < feats, spreads, 1.0)
        centers_ref[...] = centers
        spreads_ref[...] = spreads
        matrix[...] = score_matrix(centers, spreads, jnp.log(weights), feats, slot)
        total[...] = jnp.zeros(total.shape, jnp.float32)

    partial = jnp.zeros(total.shape, jnp.float32)
    for start in range(0, cols, chunk):
        shares, sums = expectation(
            gathered(features_ref, start, chunk, slot), matrix[...], components
        )
        partial = partial + sums
        for k in range(chunk):
            turned[pl.ds(start + k, components, stride=cols), :] = shares[
                :, k * samples : (k + 1) * samples
            ]
    total[...] += partial
    for component in range(components):
        posterior_ref[0, component] = turned[pl.ds(component * cols, cols), :].astype(jnp.bfloat16)

    @pl.when(row == pl.num_programs(0) - 1)
    def _():
        sums_ref[...] = fold_sums(total[...], components, slot)


def exchange(values, axis, pairs):
    return lax.ppermute(values, axis, [p for a, b in pairs for p in ((a, b), (b, a))])


def group_sum(values):
    axes = ("inline", "xline")
    count = lax.axis_size("inline") * lax.axis_size("xline")
    if count & (count - 1):
        return lax.psum(values, axes)
    step = 1
    while step < count:
        radix = min(4, count // step)
        arrived = [
            lax.ppermute(values, axes, [(i, i ^ (step * d)) for i in range(count)])
            for d in range(1, radix)
        ]
        if radix == 4:
            values = (values + arrived[0]) + (arrived[1] + arrived[2])
        else:
            values = values + arrived[0]
        step *= radix
    return values


def per_device(traces, directions, init_means, init_variances, init_weights):
    rows, cols, samples = traces.shape
    orients = directions.shape[0]
    components = init_weights.shape[0]
    feats = 2 * orients
    slot = round_up(feats + 1, SUBLANES)
    window = round_up(rows + 2 * HALF, 16)
    inlines = lax.axis_size("inline")
    if lax.axis_size("xline") != 2 or samples != LANES or rows < HALF:
        raise ValueError("unsupported sizes")

    core_pairs = [(0, 1)]
    other = exchange(traces, "xline", core_pairs)
    swap_one = exchange(traces, "inline", [(i, i + 1) for i in range(0, inlines - 1, 2)])
    swap_two = exchange(traces, "inline", [(i, i + 1) for i in range(1, inlines - 1, 2)])
    swap_one_other = exchange(swap_one, "xline", core_pairs)
    swap_two_other = exchange(swap_two, "xline", core_pairs)

    taps = tap_table(directions).astype(jnp.float32)
    taps = jnp.concatenate([taps[:, :2], taps[:, 2:, :, ::-1]], axis=1)
    taps = jnp.pad(taps.reshape(orients * 6, TAPS), ((0, 0), (0, 2 * LANES - TAPS)))
    vmem = pl.BlockSpec(memory_space=pltpu.VMEM)
    time_mats, xline_mats, inline_mats = pl.pallas_call(
        functools.partial(matrices_kernel, (orients, samples, cols, rows, window)),
        out_shape=(
            jax.ShapeDtypeStruct((orients, samples, 2 * samples), jnp.bfloat16),
            jax.ShapeDtypeStruct((orients, 4 * cols, 4 * cols), jnp.bfloat16),
            jax.ShapeDtypeStruct((orients, 2 * rows, 2 * window), jnp.bfloat16),
        ),
        in_specs=[vmem],
        out_specs=(vmem, vmem, vmem),
        name="filter_matrices",
        cost_estimate=pl.CostEstimate(flops=0, bytes_accessed=4_000_000, transcendentals=0),
    )(taps)

    whole = lambda *shape: pl.BlockSpec(shape, lambda o: (0,) * len(shape))
    chunk = 4
    features, sums = pl.pallas_call(
        functools.partial(
            features_kernel, (orients, samples, cols, rows, window, components, chunk)
        ),
        grid=(orients,),
        out_shape=(
            jax.ShapeDtypeStruct((rows * cols * slot, samples), jnp.float32),
            jax.ShapeDtypeStruct((components, LANES), jnp.float32),
        ),
        in_specs=[whole(rows, cols, samples)] * 6
        + [
            pl.BlockSpec((1, samples, 2 * samples), lambda o: (o, 0, 0)),
            pl.BlockSpec((1, 4 * cols, 4 * cols), lambda o: (o, 0, 0)),
            pl.BlockSpec((1, 2 * rows, 2 * window), lambda o: (o, 0, 0)),
            whole(components, feats),
            whole(components, feats),
            whole(1, components),
        ],
        out_specs=(whole(rows * cols * slot, samples), whole(components, LANES)),
        scratch_shapes=[
            pltpu.VMEM((window * 2 * cols, samples), jnp.bfloat16),
            pltpu.VMEM((4 * cols * window, samples), jnp.float32),
            pltpu.VMEM((2 * components, LANES), jnp.float32),
            pltpu.VMEM((2 * components, 6 * slot), jnp.float32),
        ],
        compiler_params=pltpu.CompilerParams(vmem_limit_bytes=40 * 2**20),
        name="features_and_first_moments",
    )(
        traces, other, swap_one, swap_one_other, swap_two, swap_two_other,
        time_mats, xline_mats, inline_mats,
        init_means, init_variances, init_weights.reshape(1, components),
    )
    sums = group_sum(sums)
    cells = inlines * rows * lax.axis_size("xline") * cols * samples
    posterior, sums, centers, spreads = pl.pallas_call(
        functools.partial(
            posterior_kernel, (orients, samples, cols, rows, components, chunk, cells)
        ),
        grid=(rows,),
        out_shape=(
            jax.ShapeDtypeStruct((rows, components, cols, samples), jnp.bfloat16),
            jax.ShapeDtypeStruct((components, LANES), jnp.float32),
            jax.ShapeDtypeStruct((components, LANES), jnp.float32),
            jax.ShapeDtypeStruct((components, LANES), jnp.float32),
        ),
        in_specs=[
            pl.BlockSpec((cols * slot, samples), lambda r: (r, 0)),
            whole(components, feats),
            whole(components, feats),
            whole(components, LANES),
        ],
        out_specs=(
            pl.BlockSpec((1, components, cols, samples), lambda r: (r, 0, 0, 0)),
            whole(components, LANES),
            whole(components, LANES),
            whole(components, LANES),
        ),
        scratch_shapes=[
            pltpu.VMEM((3 * components, 6 * slot), jnp.bfloat16),
            pltpu.VMEM((2 * components, 6 * slot), jnp.float32),
            pltpu.VMEM((components * cols, samples), jnp.float32),
        ],
        compiler_params=pltpu.CompilerParams(vmem_limit_bytes=40 * 2**20),
        name="posterior_and_second_moments",
    )(features, init_means, init_variances, sums)
    sums = group_sum(sums)
    mass = sums[:, feats : feats + 1]
    first = sums[:, :feats]
    second = sums[:, slot : slot + feats]
    centers, spreads = centers[:, :feats], spreads[:, :feats]
    moved = (first + centers) / (mass + 1.0)
    centred = second - 2.0 * moved * first + moved * moved * mass
    final_spreads = (centred + spreads) / (mass + 1.0)
    return posterior, moved, final_spreads, (mass[:, 0] + 1.0) / (cells + components)


def solution(mesh):
    in_specs = (P(("slab", "inline"), "xline", None), P(), P(), P(), P())
    out_specs = (
        P(("slab", "inline"), None, "xline", None),
        P("slab", None),
        P("slab", None),
        P("slab"),
    )
    return jax.shard_map(
        per_device, mesh=mesh, in_specs=in_specs, out_specs=out_specs, check_vma=False
    )
```

```python
import functools
import math

import jax
import jax.numpy as jnp
from jax import lax
from jax.experimental import pallas as pl
from jax.experimental.pallas import tpu as pltpu
from jax.sharding import PartitionSpec as P

TAPS = 31
HALF = 15
AZIMUTHS = 8
DIPS = 4
LANES = 128
SUBLANES = 8

eps_mag = 0.01
wavenumber = math.pi / 4.0


def round_up(value, step):
    return (value + step - 1) // step * step


def split(values, count):
    pieces = []
    for _ in range(count):
        pieces.append(values.astype(jnp.bfloat16))
        values = values - pieces[-1].astype(jnp.float32)
    return pieces


def tap_lines(directions_ref, orients):
    shape = (round_up(orients, SUBLANES), LANES)
    rows = lax.broadcasted_iota(jnp.int32, shape, 0)
    lanes = lax.broadcasted_iota(jnp.int32, shape, 1)
    direction = jnp.zeros(shape, jnp.int32)
    for orient in range(orients):
        direction = jnp.where(rows == orient, directions_ref[orient], direction)
    azimuth = lax.rem(direction, AZIMUTHS).astype(jnp.float32) * (math.pi / AZIMUTHS)
    dip_angle = (lax.div(direction, AZIMUTHS) + 1).astype(jnp.float32) * (math.pi / (2 * DIPS + 2))
    offsets = lanes.astype(jnp.float32) - HALF
    used = lanes < TAPS
    width_scale = HALF / 3.0
    envelope = jnp.exp(-offsets * offsets / (2.0 * width_scale * width_scale))
    envelope = jnp.where(used, envelope, 0.0)
    envelope = envelope / jnp.sqrt(jnp.sum(envelope * envelope, axis=1, keepdims=True))
    sine = jnp.sin(dip_angle)
    lines = []
    for wave, sign in (
        (wavenumber * (sine * jnp.cos(azimuth)), 1.0),
        (wavenumber * (sine * jnp.sin(azimuth)), 1.0),
        (wavenumber * jnp.cos(dip_angle), -1.0),
    ):
        phase = wave * (offsets * sign)
        pair = (envelope * jnp.cos(phase), envelope * jnp.sin(phase))
        lines.append([part.astype(jnp.bfloat16).astype(jnp.float32) for part in pair])
    return lines


def matrices_kernel(dims, directions_ref, time_ref, xline_ref, inline_ref):
    orients, samples, cols, rows, window = dims
    side = lax.axis_index("xline")
    lanes = lax.broadcasted_iota(jnp.int32, (SUBLANES, LANES), 1)[:1]
    lines = tap_lines(directions_ref, orients)

    def sheared(line, count, shift, width):
        if width > LANES:
            line = jnp.concatenate([line, jnp.zeros((1, width - LANES), jnp.float32)], axis=1)
        wide = jnp.broadcast_to(line, (count, width))
        return pltpu.roll(wide, shift % width, 1, stride=1, stride_axis=0)

    for orient in range(orients):
        line = lambda axis, part: lines[axis][part][orient : orient + 1]
        for part in range(2):
            time_ref[orient, :, part * samples : (part + 1) * samples] = sheared(
                line(2, part), samples, 2 * samples - HALF, 2 * samples
            )[:, :samples].astype(jnp.bfloat16)

        def xline_half(part, half, slot):
            shift = LANES - HALF + slot * cols
            if half:
                moved = jnp.where(
                    side == 0,
                    sheared(line(1, part), cols, shift + LANES - cols, LANES),
                    sheared(line(1, part), cols, shift + cols, LANES),
                )
            else:
                moved = sheared(line(1, part), cols, shift, LANES)
            return jnp.where((lanes >= slot * cols) & (lanes < (slot + 1) * cols), moved, 0.0)

        cosine = [xline_half(0, 0, p * 2) + xline_half(0, 1, p * 2 + 1) for p in range(2)]
        sine = [xline_half(1, 0, p * 2) + xline_half(1, 1, p * 2 + 1) for p in range(2)]
        xline_ref[orient] = jnp.concatenate(
            [
                cosine[0] - sine[1],
                sine[0] + cosine[1],
                cosine[0] + sine[1],
                sine[0] - cosine[1],
            ],
            axis=0,
        )[:, : 4 * cols].astype(jnp.bfloat16)

        def inline_part(part, slot):
            moved = sheared(line(0, part), rows, slot * window, LANES)
            return jnp.where((lanes >= slot * window) & (lanes < (slot + 1) * window), moved, 0.0)

        inline_ref[orient] = jnp.concatenate(
            [
                inline_part(0, 0) - inline_part(1, 1),
                inline_part(1, 0) + inline_part(0, 1),
            ],
            axis=0,
        )[:, : 2 * window].astype(jnp.bfloat16)


def score_matrix(centers, spreads, log_weights, feats, slot, levels):
    lanes = lax.broadcasted_iota(jnp.int32, centers.shape, 1)
    real = lanes < feats
    inverse = 1.0 / spreads
    widen = lambda values, count: [p.astype(jnp.float32) for p in split(values, count)]
    linear = widen(centers * inverse, levels)
    square = widen(-0.5 * inverse, levels)
    kept_linear, kept_square = sum(linear), sum(square)
    terms = jnp.log(2.0 * math.pi * spreads) - 0.5 * kept_linear * (kept_linear / kept_square)
    constant = log_weights - 0.5 * jnp.sum(jnp.where(real, terms, 0.0), axis=1, keepdims=True)
    constants = widen(constant, 3)
    groups = []
    for level in range(levels):
        first = jnp.where(real, linear[level], 0.0)
        first = jnp.where(lanes == feats, constants[level], first)
        if level == 0 and levels == 2:
            first = jnp.where(lanes == feats + 1, constants[2], first)
        both = first + pltpu.roll(jnp.where(real, square[level], 0.0), slot, 1)
        both = jnp.concatenate([both, jnp.zeros_like(both)], axis=1)
        groups.append(both + pltpu.roll(both, 2 * slot, 1) + pltpu.roll(both, 4 * slot, 1))
    return jnp.concatenate(groups, axis=0)[:, : 6 * slot].astype(jnp.bfloat16)


def score_stage(features, matrix, data_ref, scores_ref, place, components):
    both = jnp.concatenate([features, features * features], axis=0)
    data = jnp.concatenate(split(both, 3), axis=0)
    data_ref[:, place] = data[: data_ref.shape[0]]
    scores = jnp.dot(matrix, data, preferred_element_type=jnp.float32)
    scores_ref[:, place] = sum(
        scores[k : k + components] for k in range(0, matrix.shape[0], components)
    )


def moment_stage(data_ref, scores_ref, place):
    scores = scores_ref[:, place]
    exponent = jnp.exp(scores - jnp.max(scores, axis=0, keepdims=True))
    shares = exponent * (1.0 / jnp.sum(exponent, axis=0, keepdims=True))
    high = shares.astype(jnp.bfloat16)
    low = (shares - high.astype(jnp.float32)).astype(jnp.bfloat16)
    sums = lax.dot_general(
        data_ref[:, place],
        jnp.concatenate([high, low], axis=0),
        (((1,), (1,)), ((), ())),
        preferred_element_type=jnp.float32,
    )
    return shares, sums


def gathered(features_ref, row, rows, first, count, slot):
    place = lambda col: (col * rows + row) * (slot + 1)
    return jnp.concatenate(
        [features_ref[pl.ds(place(first + k), slot), :] for k in range(count)], axis=1
    )


def fold_sums(total, components, slot):
    both = total[:, :components] + total[:, components:]
    both = both[: 2 * slot] + both[2 * slot :]
    return jnp.concatenate(
        [both, jnp.zeros((LANES - 2 * slot, components), jnp.float32)], axis=0
    ).T


def features_kernel(dims, *refs):
    orients, samples, cols, rows, window, components, chunk, unit = dims
    halves, refs = refs[:6], refs[6:]
    time_ref, xline_ref, inline_ref, means_ref, variances_ref, weights_ref = refs[:6]
    features_ref, sums_ref, traces, across, params, total, data, scores, own, arrived = refs[6:]
    feats = 2 * orients
    slot = round_up(feats + 2, SUBLANES)
    orient = pl.program_id(0)
    @pl.when(orient == 0)
    def _():
        own_copy = pltpu.make_async_copy(halves[0], own, arrived)
        own_copy.start()
        own_copy.wait()
        other, swap_one, swap_one_other, swap_two, swap_two_other = halves[1:]
        even = lax.rem(lax.axis_index("inline"), 2) == 0

        def put(place, near, far):
            traces[pl.ds(place * 2 * cols, 2 * cols), :] = jnp.concatenate(
                [near.astype(jnp.float32), far.astype(jnp.float32)], axis=0
            ).astype(jnp.bfloat16)

        for row in range(rows):
            put(HALF + row, own[row], other[row])
            one = swap_one[row].astype(jnp.float32)
            one_far = swap_one_other[row].astype(jnp.float32)
            two = swap_two[row].astype(jnp.float32)
            two_far = swap_two_other[row].astype(jnp.float32)
            if row >= rows - HALF:
                put(row - (rows - HALF), jnp.where(even, two, one), jnp.where(even, two_far, one_far))
            if row < HALF:
                put(HALF + rows + row, jnp.where(even, one, two), jnp.where(even, one_far, two_far))
        for place in range(rows + 2 * HALF, window):
            traces[pl.ds(place * 2 * cols, 2 * cols), :] = jnp.zeros(
                (2 * cols, samples), jnp.bfloat16
            )
        for extra in range(feats, slot):
            filler = jnp.full((rows, samples), 1.0 if extra < feats + 2 else 0.0, jnp.float32)
            for col in range(cols):
                place = col * rows * (slot + 1) + extra
                features_ref[pl.ds(place, rows, stride=slot + 1), :] = filler

    lines = 2 * cols
    apart = window + 1
    group = window
    for pair in range(window // 2):
        if pair * 2 % group == 0:
            block = traces[pl.ds(pair * 2 * lines, group * lines), :]
            band = jnp.dot(block, time_ref[0], preferred_element_type=jnp.float32)
            band = band.astype(jnp.bfloat16)

        def piece(k, p):
            first = (pair * 2 % group + k) * lines
            return band[first : first + lines, p * samples : (p + 1) * samples]

        stacked = jnp.concatenate(
            [jnp.concatenate([piece(k, 0), piece(k, 1)], axis=0) for k in range(2)], axis=1
        )
        crossed = jnp.dot(xline_ref[0], stacked, preferred_element_type=jnp.float32)
        for k in range(2):
            across[pl.ds(2 * pair + k, 4 * cols, stride=apart), :] = crossed[
                :, k * samples : (k + 1) * samples
            ]
    for polarity in range(2):
        for col in range(0, cols, 2):

            def taken(k, part):
                place = ((polarity * 2 + part) * cols + col + k) * apart
                return across[pl.ds(place, window), :]

            stacked = jnp.concatenate(
                [jnp.concatenate([taken(k, 0), taken(k, 1)], axis=0) for k in range(2)], axis=1
            ).astype(jnp.bfloat16)
            found = jnp.dot(inline_ref[0], stacked, preferred_element_type=jnp.float32)
            real_part, imag_part = found[:rows], found[rows:]
            power = real_part * real_part + imag_part * imag_part + eps_mag
            size = power * lax.rsqrt(power)
            for k in range(2):
                place = (col + k) * rows * (slot + 1) + 2 * orient + polarity
                features_ref[pl.ds(place, rows, stride=slot + 1), :] = size[
                    :, k * samples : (k + 1) * samples
                ]

    @pl.when(orient == orients - 1)
    def _():
        params[...] = jnp.ones(params.shape, jnp.float32)
        params[:components, :feats] = means_ref[...]
        params[components:, :feats] = variances_ref[...]
        row_ids = lax.broadcasted_iota(jnp.int32, (components, 1), 0)
        weights = jnp.ones((components, 1), jnp.float32)
        for component in range(components):
            weights = jnp.where(row_ids == component, weights_ref[component], weights)
        log_weights = jnp.log(weights)
        matrix = score_matrix(
            params[:components], params[components:], log_weights, feats, slot, 3
        )
        total[...] = jnp.zeros(total.shape, jnp.float32)

        data[...] = jnp.zeros(data.shape, jnp.bfloat16)
        scores[...] = jnp.zeros(scores.shape, jnp.float32)

        @pl.loop(0, rows // unit + 1)
        def _(step):
            block = jnp.minimum(step, rows // unit - 1)
            partial = jnp.zeros(total.shape, jnp.float32)
            for start in range(0, unit * cols, chunk):
                place = slice(start * samples, (start + chunk) * samples)
                partial = partial + moment_stage(data, scores, place)[1]
                lines = gathered(features_ref, block * unit + start // cols, rows, start % cols, chunk, slot)
                score_stage(lines, matrix, data, scores, place, components)
            total[...] += partial

        sums_ref[...] = fold_sums(total[...], components, slot)


def new_params(sums, centers, spreads, feats, slot, cells):
    components = centers.shape[0]
    mass = sums[:, feats : feats + 1]
    first = sums
    second = pltpu.roll(sums, LANES - slot, 1)
    scale = 1.0 / (mass + 1.0)
    moved = (first + centers) * scale
    centred = second - 2.0 * moved * first + moved * moved * mass
    return moved, (centred + spreads) * scale, (mass + 1.0) / (cells + components)


def posterior_kernel(dims, *refs):
    orients, samples, cols, rows, components, chunk, unit, cells = dims
    features_ref, means_ref, variances_ref, before_ref = refs[:4]
    posterior_ref, sums_ref, centers_ref, spreads_ref, matrix, total, turned, data, scores = refs[4:]
    feats = 2 * orients
    slot = round_up(feats + 2, SUBLANES)
    step = pl.program_id(0)
    block = jnp.minimum(step, rows // unit - 1)

    @pl.when(step == 0)
    def _():
        centers_ref[...] = jnp.zeros(centers_ref.shape, jnp.float32)
        spreads_ref[...] = jnp.ones(spreads_ref.shape, jnp.float32)
        centers_ref[:, :feats] = means_ref[...]
        spreads_ref[:, :feats] = variances_ref[...]
        centers, spreads, weights = new_params(
            before_ref[...], centers_ref[...], spreads_ref[...], feats, slot, cells
        )
        lanes = lax.broadcasted_iota(jnp.int32, centers.shape, 1)
        centers = jnp.where(lanes < feats, centers, 0.0)
        spreads = jnp.where(lanes < feats, spreads, 1.0)
        centers_ref[...] = centers
        spreads_ref[...] = spreads
        matrix[...] = score_matrix(centers, spreads, jnp.log(weights), feats, slot, 2)
        total[...] = jnp.zeros(total.shape, jnp.float32)
        data[...] = jnp.zeros(data.shape, jnp.bfloat16)
        scores[...] = jnp.zeros(scores.shape, jnp.float32)

    partial = jnp.zeros(total.shape, jnp.float32)
    for start in range(0, unit * cols, chunk):
        place = slice(start * samples, (start + chunk) * samples)
        which, col = start // cols, start % cols
        shares, sums = moment_stage(data, scores, place)
        lines = gathered(features_ref, block * unit + which, rows, col, chunk, slot)
        score_stage(lines, matrix[...], data, scores, place, components)
        partial = partial + sums
        for k in range(chunk):
            turned[which, pl.ds(col + k, components, stride=cols + 1), :] = shares[
                :, k * samples : (k + 1) * samples
            ]
    total[...] += partial
    for which in range(unit):
        for component in range(components):
            posterior_ref[which, component] = turned[
                which, pl.ds(component * (cols + 1), cols), :
            ].astype(jnp.bfloat16)

    @pl.when(step == pl.num_programs(0) - 1)
    def _():
        sums_ref[...] = fold_sums(total[...], components, slot)


def exchange(values, axis, pairs):
    return lax.ppermute(values, axis, [p for a, b in pairs for p in ((a, b), (b, a))])


def group_sum(values):
    axes = ("inline", "xline")
    count = lax.axis_size("inline") * lax.axis_size("xline")
    if count & (count - 1):
        return lax.psum(values, axes)
    step = 1
    while step < count:
        radix = min(4, count // step)
        arrived = [
            lax.ppermute(values, axes, [(i, i ^ (step * d)) for i in range(count)])
            for d in range(1, radix)
        ]
        if radix == 4:
            values = (values + arrived[0]) + (arrived[1] + arrived[2])
        else:
            values = values + arrived[0]
        step *= radix
    return values


def per_device(traces, directions, init_means, init_variances, init_weights):
    rows, cols, samples = traces.shape
    orients = directions.shape[0]
    components = init_weights.shape[0]
    feats = 2 * orients
    slot = round_up(feats + 2, SUBLANES)
    window = round_up(rows + 2 * HALF, 16)
    inlines = lax.axis_size("inline")
    if lax.axis_size("xline") != 2 or samples != LANES or rows < HALF:
        raise ValueError("unsupported sizes")

    core_pairs = [(0, 1)]
    other = exchange(traces, "xline", core_pairs)
    swap_one = exchange(traces, "inline", [(i, i + 1) for i in range(0, inlines - 1, 2)])
    swap_two = exchange(traces, "inline", [(i, i + 1) for i in range(1, inlines - 1, 2)])
    vmem = pl.BlockSpec(memory_space=pltpu.VMEM)
    time_mats, xline_mats, inline_mats = pl.pallas_call(
        functools.partial(matrices_kernel, (orients, samples, cols, rows, window)),
        out_shape=(
            jax.ShapeDtypeStruct((orients, samples, 2 * samples), jnp.bfloat16),
            jax.ShapeDtypeStruct((orients, 4 * cols, 4 * cols), jnp.bfloat16),
            jax.ShapeDtypeStruct((orients, 2 * rows, 2 * window), jnp.bfloat16),
        ),
        in_specs=[pl.BlockSpec(memory_space=pltpu.SMEM)],
        out_specs=(vmem, vmem, vmem),
        compiler_params=pltpu.CompilerParams(vmem_limit_bytes=8 * 2**20),
        name="filter_matrices",
        cost_estimate=pl.CostEstimate(flops=0, bytes_accessed=4_000_000, transcendentals=0),
    )(directions)

    swap_one, swap_two, time_mats, xline_mats, inline_mats = lax.optimization_barrier(
        (swap_one, swap_two, time_mats, xline_mats, inline_mats)
    )
    swap_one_other = exchange(swap_one, "xline", core_pairs)
    swap_two_other = exchange(swap_two, "xline", core_pairs)

    whole = lambda *shape: pl.BlockSpec(shape, lambda o: (0,) * len(shape))
    chunk = 6
    unit = 2 if rows % 2 == 0 else 1
    features, sums = pl.pallas_call(
        functools.partial(
            features_kernel, (orients, samples, cols, rows, window, components, chunk, unit)
        ),
        grid=(orients,),
        out_shape=(
            jax.ShapeDtypeStruct((rows * cols * (slot + 1), samples), jnp.float32),
            jax.ShapeDtypeStruct((components, LANES), jnp.float32),
        ),
        in_specs=[pl.BlockSpec(memory_space=pltpu.HBM)]
        + [whole(rows, cols, samples)] * 5
        + [
            pl.BlockSpec((1, samples, 2 * samples), lambda o: (o, 0, 0)),
            pl.BlockSpec((1, 4 * cols, 4 * cols), lambda o: (o, 0, 0)),
            pl.BlockSpec((1, 2 * rows, 2 * window), lambda o: (o, 0, 0)),
            whole(components, feats),
            whole(components, feats),
            pl.BlockSpec(memory_space=pltpu.SMEM),
        ],
        out_specs=(whole(rows * cols * (slot + 1), samples), whole(components, LANES)),
        scratch_shapes=[
            pltpu.VMEM((window * 2 * cols, samples), jnp.bfloat16),
            pltpu.VMEM((4 * cols * (window + 1), samples), jnp.float32),
            pltpu.VMEM((2 * components, LANES), jnp.float32),
            pltpu.VMEM((4 * slot, 2 * components), jnp.float32),
            pltpu.VMEM((4 * slot, unit * cols * samples), jnp.bfloat16),
            pltpu.VMEM((components, unit * cols * samples), jnp.float32),
            pltpu.VMEM((rows, cols, samples), jnp.bfloat16),
            pltpu.SemaphoreType.DMA,
        ],
        compiler_params=pltpu.CompilerParams(vmem_limit_bytes=40 * 2**20),
        name="features_and_first_moments",
    )(
        traces, other, swap_one, swap_one_other, swap_two, swap_two_other,
        time_mats, xline_mats, inline_mats,
        init_means, init_variances, init_weights,
    )
    sums = group_sum(sums)
    cells = inlines * rows * lax.axis_size("xline") * cols * samples
    posterior, sums, centers, spreads = pl.pallas_call(
        functools.partial(
            posterior_kernel, (orients, samples, cols, rows, components, chunk, unit, cells)
        ),
        grid=(rows // unit + 1,),
        out_shape=(
            jax.ShapeDtypeStruct((rows, components, cols, samples), jnp.bfloat16),
            jax.ShapeDtypeStruct((components, LANES), jnp.float32),
            jax.ShapeDtypeStruct((components, LANES), jnp.float32),
            jax.ShapeDtypeStruct((components, LANES), jnp.float32),
        ),
        in_specs=[
            whole(rows * cols * (slot + 1), samples),
            whole(components, feats),
            whole(components, feats),
            whole(components, LANES),
        ],
        out_specs=(
            pl.BlockSpec((unit, components, cols, samples), lambda r: (jnp.maximum(r - 1, 0), 0, 0, 0)),
            whole(components, LANES),
            whole(components, LANES),
            whole(components, LANES),
        ),
        scratch_shapes=[
            pltpu.VMEM((2 * components, 6 * slot), jnp.bfloat16),
            pltpu.VMEM((4 * slot, 2 * components), jnp.float32),
            pltpu.VMEM((unit, components * (cols + 1), samples), jnp.float32),
            pltpu.VMEM((4 * slot, unit * cols * samples), jnp.bfloat16),
            pltpu.VMEM((components, unit * cols * samples), jnp.float32),
        ],
        compiler_params=pltpu.CompilerParams(vmem_limit_bytes=40 * 2**20),
        name="posterior_and_second_moments",
    )(features, init_means, init_variances, sums)
    sums = group_sum(sums)
    mass = sums[:, feats : feats + 1]
    first = sums[:, :feats]
    second = sums[:, slot : slot + feats]
    centers, spreads = centers[:, :feats], spreads[:, :feats]
    moved = (first + centers) / (mass + 1.0)
    centred = second - 2.0 * moved * first + moved * moved * mass
    final_spreads = (centred + spreads) / (mass + 1.0)
    return posterior, moved, final_spreads, (mass[:, 0] + 1.0) / (cells + components)


def solution(mesh):
    in_specs = (P(("slab", "inline"), "xline", None), P(), P(), P(), P())
    out_specs = (
        P(("slab", "inline"), None, "xline", None),
        P("slab", None),
        P("slab", None),
        P("slab"),
    )
    return jax.shard_map(
        per_device, mesh=mesh, in_specs=in_specs, out_specs=out_specs, check_vma=False
    )
```

```python
import functools
import math

import jax
import jax.numpy as jnp
from jax import lax
from jax.experimental import pallas as pl
from jax.experimental.pallas import tpu as pltpu
from jax.sharding import PartitionSpec as P

TAPS = 31
HALF = 15
AZIMUTHS = 8
DIPS = 4
LANES = 128
SUBLANES = 8

eps_mag = 0.01
wavenumber = math.pi / 4.0


def round_up(value, step):
    return (value + step - 1) // step * step


def split(values, count):
    pieces = []
    for _ in range(count):
        pieces.append(values.astype(jnp.bfloat16))
        values = values - pieces[-1].astype(jnp.float32)
    return pieces


def tap_lines(directions_ref, orients):
    shape = (round_up(orients, SUBLANES), LANES)
    rows = lax.broadcasted_iota(jnp.int32, shape, 0)
    lanes = lax.broadcasted_iota(jnp.int32, shape, 1)
    direction = jnp.zeros(shape, jnp.int32)
    for orient in range(orients):
        direction = jnp.where(rows == orient, directions_ref[orient], direction)
    azimuth = lax.rem(direction, AZIMUTHS).astype(jnp.float32) * (math.pi / AZIMUTHS)
    dip_angle = (lax.div(direction, AZIMUTHS) + 1).astype(jnp.float32) * (math.pi / (2 * DIPS + 2))
    offsets = lanes.astype(jnp.float32) - HALF
    used = lanes < TAPS
    width_scale = HALF / 3.0
    envelope = jnp.exp(-offsets * offsets / (2.0 * width_scale * width_scale))
    envelope = jnp.where(used, envelope, 0.0)
    envelope = envelope / jnp.sqrt(jnp.sum(envelope * envelope, axis=1, keepdims=True))
    sine = jnp.sin(dip_angle)
    lines = []
    for wave, sign in (
        (wavenumber * (sine * jnp.cos(azimuth)), 1.0),
        (wavenumber * (sine * jnp.sin(azimuth)), 1.0),
        (wavenumber * jnp.cos(dip_angle), -1.0),
    ):
        phase = wave * (offsets * sign)
        pair = (envelope * jnp.cos(phase), envelope * jnp.sin(phase))
        lines.append([part.astype(jnp.bfloat16).astype(jnp.float32) for part in pair])
    return lines


def matrices_kernel(dims, directions_ref, own_ref, time_ref, xline_ref, inline_ref, kept_ref):
    orients, samples, cols, rows, window = dims
    side = lax.axis_index("xline")
    lanes = lax.broadcasted_iota(jnp.int32, (SUBLANES, LANES), 1)[:1]
    lines = tap_lines(directions_ref, orients)
    kept_ref[...] = own_ref[...]

    def sheared(line, count, shift, width):
        if width > LANES:
            line = jnp.concatenate([line, jnp.zeros((1, width - LANES), jnp.float32)], axis=1)
        wide = jnp.broadcast_to(line, (count, width))
        return pltpu.roll(wide, shift % width, 1, stride=1, stride_axis=0)

    for orient in range(orients):
        line = lambda axis, part: lines[axis][part][orient : orient + 1]
        for part in range(2):
            time_ref[orient, :, part * samples : (part + 1) * samples] = sheared(
                line(2, part), samples, 2 * samples - HALF, 2 * samples
            )[:, :samples].astype(jnp.bfloat16)

        def xline_half(part, half, slot):
            shift = LANES - HALF + slot * cols
            if half:
                moved = jnp.where(
                    side == 0,
                    sheared(line(1, part), cols, shift + LANES - cols, LANES),
                    sheared(line(1, part), cols, shift + cols, LANES),
                )
            else:
                moved = sheared(line(1, part), cols, shift, LANES)
            return jnp.where((lanes >= slot * cols) & (lanes < (slot + 1) * cols), moved, 0.0)

        cosine = [xline_half(0, 0, p * 2) + xline_half(0, 1, p * 2 + 1) for p in range(2)]
        sine = [xline_half(1, 0, p * 2) + xline_half(1, 1, p * 2 + 1) for p in range(2)]
        xline_ref[orient] = jnp.concatenate(
            [
                cosine[0] - sine[1],
                sine[0] + cosine[1],
                cosine[0] + sine[1],
                sine[0] - cosine[1],
            ],
            axis=0,
        )[:, : 4 * cols].astype(jnp.bfloat16)

        def inline_part(part, slot):
            moved = sheared(line(0, part), rows, slot * window, LANES)
            return jnp.where((lanes >= slot * window) & (lanes < (slot + 1) * window), moved, 0.0)

        inline_ref[orient] = jnp.concatenate(
            [
                inline_part(0, 0) - inline_part(1, 1),
                inline_part(1, 0) + inline_part(0, 1),
            ],
            axis=0,
        )[:, : 2 * window].astype(jnp.bfloat16)


def score_matrix(centers, spreads, log_weights, feats, slot, levels):
    lanes = lax.broadcasted_iota(jnp.int32, centers.shape, 1)
    real = lanes < feats
    inverse = 1.0 / spreads
    widen = lambda values, count: [p.astype(jnp.float32) for p in split(values, count)]
    linear = widen(centers * inverse, levels)
    square = widen(-0.5 * inverse, levels)
    kept_linear, kept_square = sum(linear), sum(square)
    terms = jnp.log(2.0 * math.pi * spreads) - 0.5 * kept_linear * (kept_linear / kept_square)
    constant = log_weights - 0.5 * jnp.sum(jnp.where(real, terms, 0.0), axis=1, keepdims=True)
    constants = widen(constant, 3)
    groups = []
    for level in range(levels):
        first = jnp.where(real, linear[level], 0.0)
        first = jnp.where(lanes == feats, constants[level], first)
        if level == 0 and levels == 2:
            first = jnp.where(lanes == feats + 1, constants[2], first)
        both = first + pltpu.roll(jnp.where(real, square[level], 0.0), slot, 1)
        both = jnp.concatenate([both, jnp.zeros_like(both)], axis=1)
        groups.append(both + pltpu.roll(both, 2 * slot, 1) + pltpu.roll(both, 4 * slot, 1))
    return jnp.concatenate(groups, axis=0)[:, : 6 * slot].astype(jnp.bfloat16)


def score_stage(features, matrix, data_ref, scores_ref, place, components):
    both = jnp.concatenate([features, features * features], axis=0)
    data = jnp.concatenate(split(both, 3), axis=0)
    data_ref[:, place] = data[: data_ref.shape[0]]
    scores = jnp.dot(matrix, data, preferred_element_type=jnp.float32)
    scores_ref[:, place] = sum(
        scores[k : k + components] for k in range(0, matrix.shape[0], components)
    )


def moment_stage(data_ref, scores_ref, place):
    scores = scores_ref[:, place]
    exponent = jnp.exp(scores - jnp.max(scores, axis=0, keepdims=True))
    shares = exponent * (1.0 / jnp.sum(exponent, axis=0, keepdims=True))
    high = shares.astype(jnp.bfloat16)
    low = (shares - high.astype(jnp.float32)).astype(jnp.bfloat16)
    sums = lax.dot_general(
        data_ref[:, place],
        jnp.concatenate([high, low], axis=0),
        (((1,), (1,)), ((), ())),
        preferred_element_type=jnp.float32,
    )
    return shares, sums


def gathered(features_ref, row, rows, first, count, slot):
    place = lambda col: (col * rows + row) * (slot + 1)
    return jnp.concatenate(
        [features_ref[pl.ds(place(first + k), slot), :] for k in range(count)], axis=1
    )


def fold_sums(total, components, slot):
    both = total[:, :components] + total[:, components:]
    both = both[: 2 * slot] + both[2 * slot :]
    return jnp.concatenate(
        [both, jnp.zeros((LANES - 2 * slot, components), jnp.float32)], axis=0
    ).T


def features_kernel(dims, *refs):
    orients, samples, cols, rows, window, components, chunk, unit = dims
    halves, refs = refs[:6], refs[6:]
    time_ref, xline_ref, inline_ref, params_ref = refs[:4]
    features_ref, sums_ref, traces, across_even, across_odd, total, data, scores = refs[4:]
    feats = 2 * orients
    slot = round_up(feats + 2, SUBLANES)
    twice = pl.program_id(0)
    @pl.when(twice == 0)
    def _():
        own, other, swap_one, swap_one_other, swap_two, swap_two_other = halves
        even = lax.rem(lax.axis_index("inline"), 2) == 0

        def put(place, near, far):
            traces[pl.ds(place * 2 * cols, 2 * cols), :] = jnp.concatenate(
                [near.astype(jnp.float32), far.astype(jnp.float32)], axis=0
            ).astype(jnp.bfloat16)

        for row in range(rows):
            put(HALF + row, own[row], other[row])
            one = swap_one[row].astype(jnp.float32)
            one_far = swap_one_other[row].astype(jnp.float32)
            two = swap_two[row].astype(jnp.float32)
            two_far = swap_two_other[row].astype(jnp.float32)
            if row >= rows - HALF:
                put(row - (rows - HALF), jnp.where(even, two, one), jnp.where(even, two_far, one_far))
            if row < HALF:
                put(HALF + rows + row, jnp.where(even, one, two), jnp.where(even, one_far, two_far))
        for place in range(rows + 2 * HALF, window):
            traces[pl.ds(place * 2 * cols, 2 * cols), :] = jnp.zeros(
                (2 * cols, samples), jnp.bfloat16
            )
        for extra in range(feats, slot):
            filler = jnp.full((rows, samples), 1.0 if extra < feats + 2 else 0.0, jnp.float32)
            for col in range(cols):
                place = col * rows * (slot + 1) + extra
                features_ref[pl.ds(place, rows, stride=slot + 1), :] = filler

    lines = 2 * cols
    apart = window + 1

    def magnitudes(orient, across, piece):
        polarity, col = piece // (cols // 2), piece % (cols // 2) * 2

        def taken(k, part):
            place = ((polarity * 2 + part) * cols + col + k) * apart
            return across[pl.ds(place, window), :]

        stacked = jnp.concatenate(
            [jnp.concatenate([taken(k, 0), taken(k, 1)], axis=0) for k in range(2)], axis=1
        ).astype(jnp.bfloat16)
        found = jnp.dot(inline_ref[orient], stacked, preferred_element_type=jnp.float32)
        real_part, imag_part = found[:rows], found[rows:]
        power = real_part * real_part + imag_part * imag_part + eps_mag
        size = power * lax.rsqrt(power)
        for k in range(2):
            place = (col + k) * rows * (slot + 1) + 2 * orient + polarity
            features_ref[pl.ds(place, rows, stride=slot + 1), :] = size[
                :, k * samples : (k + 1) * samples
            ]

    def filtered(which, across, before, across_before):
        band = jnp.dot(traces[...], time_ref[which], preferred_element_type=jnp.float32)
        band = band.astype(jnp.bfloat16)
        done = 0
        for pair in range(window // 2):

            def piece(k, p):
                first = (pair * 2 + k) * lines
                return band[first : first + lines, p * samples : (p + 1) * samples]

            stacked = jnp.concatenate(
                [jnp.concatenate([piece(k, 0), piece(k, 1)], axis=0) for k in range(2)], axis=1
            )
            crossed = jnp.dot(xline_ref[which], stacked, preferred_element_type=jnp.float32)
            for k in range(2):
                across[pl.ds(2 * pair + k, 4 * cols, stride=apart), :] = crossed[
                    :, k * samples : (k + 1) * samples
                ]
            until = cols * (pair + 1) // (window // 2)
            for other in range(done, until):
                magnitudes(before, across_before, other)
            done = until

    filtered(0, across_even, jnp.maximum(2 * twice - 1, 0), across_odd)
    filtered(1, across_odd, 2 * twice, across_even)

    @pl.when(twice == orients // 2 - 1)
    def _():
        for piece in range(cols):
            magnitudes(orients - 1, across_odd, piece)

    @pl.when(twice == orients // 2 - 1)
    def _():
        matrix = score_matrix(
            params_ref[:components],
            params_ref[components : 2 * components],
            jnp.log(params_ref[2 * components :, :1]),
            feats, slot, 3,
        )
        total[...] = jnp.zeros(total.shape, jnp.float32)

        data[...] = jnp.zeros(data.shape, jnp.bfloat16)
        scores[...] = jnp.zeros(scores.shape, jnp.float32)

        @pl.loop(0, rows // unit + 1)
        def _(step):
            block = jnp.minimum(step, rows // unit - 1)
            partial = jnp.zeros(total.shape, jnp.float32)
            for start in range(0, unit * cols, chunk):
                place = slice(start * samples, (start + chunk) * samples)
                partial = partial + moment_stage(data, scores, place)[1]
                lines = gathered(features_ref, block * unit + start // cols, rows, start % cols, chunk, slot)
                score_stage(lines, matrix, data, scores, place, components)
            total[...] += partial

        sums_ref[...] = fold_sums(total[...], components, slot)


def new_params(sums, centers, spreads, feats, slot, cells):
    components = centers.shape[0]
    mass = sums[:, feats : feats + 1]
    first = sums
    second = pltpu.roll(sums, LANES - slot, 1)
    scale = 1.0 / (mass + 1.0)
    moved = (first + centers) * scale
    centred = second - 2.0 * moved * first + moved * moved * mass
    return moved, (centred + spreads) * scale, (mass + 1.0) / (cells + components)


def posterior_kernel(dims, *refs):
    orients, samples, cols, rows, components, chunk, unit, cells = dims
    features_ref, params_ref, before_ref = refs[:3]
    posterior_ref, sums_ref, centers_ref, spreads_ref, matrix, total, turned, data, scores = refs[3:]
    feats = 2 * orients
    slot = round_up(feats + 2, SUBLANES)
    step = pl.program_id(0)
    block = jnp.minimum(step, rows // unit - 1)

    @pl.when(step == 0)
    def _():
        centers, spreads, weights = new_params(
            before_ref[...],
            params_ref[:components],
            params_ref[components : 2 * components],
            feats, slot, cells,
        )
        lanes = lax.broadcasted_iota(jnp.int32, centers.shape, 1)
        centers = jnp.where(lanes < feats, centers, 0.0)
        spreads = jnp.where(lanes < feats, spreads, 1.0)
        centers_ref[...] = centers
        spreads_ref[...] = spreads
        matrix[...] = score_matrix(centers, spreads, jnp.log(weights), feats, slot, 2)
        total[...] = jnp.zeros(total.shape, jnp.float32)
        data[...] = jnp.zeros(data.shape, jnp.bfloat16)
        scores[...] = jnp.zeros(scores.shape, jnp.float32)

    partial = jnp.zeros(total.shape, jnp.float32)
    for start in range(0, unit * cols, chunk):
        place = slice(start * samples, (start + chunk) * samples)
        which, col = start // cols, start % cols
        shares, sums = moment_stage(data, scores, place)
        lines = gathered(features_ref, block * unit + which, rows, col, chunk, slot)
        score_stage(lines, matrix[...], data, scores, place, components)
        partial = partial + sums
        for k in range(chunk):
            turned[which, pl.ds(col + k, components, stride=cols + 1), :] = shares[
                :, k * samples : (k + 1) * samples
            ]
    total[...] += partial
    for which in range(unit):
        for component in range(components):
            posterior_ref[which, component] = turned[
                which, pl.ds(component * (cols + 1), cols), :
            ].astype(jnp.bfloat16)

    @pl.when(step == pl.num_programs(0) - 1)
    def _():
        sums_ref[...] = fold_sums(total[...], components, slot)


def update_kernel(dims, sums_ref, centers_ref, spreads_ref, means_ref, variances_ref, weights_ref):
    feats, slot, cells = dims
    components = sums_ref.shape[0]
    rest = jnp.zeros((LANES - 3 * components, LANES), jnp.float32)
    turned = jnp.concatenate(
        [sums_ref[...], centers_ref[...], spreads_ref[...], rest], axis=0
    ).T
    part = lambda first, group: turned[
        first : first + feats, group * components : (group + 1) * components
    ]
    mass = turned[feats : feats + 1, :components]
    first, second, centers, spreads = part(0, 0), part(slot, 0), part(0, 1), part(0, 2)
    moved = (first + centers) / (mass + 1.0)
    centred = second - 2.0 * moved * first + moved * moved * mass
    means_ref[...] = moved
    variances_ref[...] = (centred + spreads) / (mass + 1.0)
    weights_ref[...] = (mass + 1.0) / (cells + components)


def exchange(values, axis, pairs):
    return lax.ppermute(values, axis, [p for a, b in pairs for p in ((a, b), (b, a))])


def group_sum(values):
    axes = ("inline", "xline")
    count = lax.axis_size("inline") * lax.axis_size("xline")
    if count & (count - 1):
        return lax.psum(values, axes)
    rounds = []
    while count > 1:
        rounds.append(min(4, count))
        count //= rounds[-1]
    for radix in rounds:
        count *= radix
    step = count
    for radix in rounds:
        step //= radix
        arrived = [
            lax.ppermute(values, axes, [(i, i ^ (step * d)) for i in range(count)])
            for d in range(1, radix)
        ]
        if radix == 4:
            values = (values + arrived[0]) + (arrived[1] + arrived[2])
        else:
            values = values + arrived[0]
    return values


def per_device(traces, directions, init_means, init_variances, init_weights):
    rows, cols, samples = traces.shape
    orients = directions.shape[0]
    components = init_weights.shape[0]
    feats = 2 * orients
    slot = round_up(feats + 2, SUBLANES)
    window = round_up(rows + 2 * HALF, 16)
    inlines = lax.axis_size("inline")
    if lax.axis_size("xline") != 2 or samples != LANES or rows < HALF or orients % 2 or cols % 2:
        raise ValueError("unsupported sizes")

    core_pairs = [(0, 1)]
    other = exchange(traces, "xline", core_pairs)
    swap_one = exchange(traces, "inline", [(i, i + 1) for i in range(0, inlines - 1, 2)])
    swap_two = exchange(traces, "inline", [(i, i + 1) for i in range(1, inlines - 1, 2)])
    vmem = pl.BlockSpec(memory_space=pltpu.VMEM)
    time_mats, xline_mats, inline_mats, own = pl.pallas_call(
        functools.partial(matrices_kernel, (orients, samples, cols, rows, window)),
        out_shape=(
            jax.ShapeDtypeStruct((orients, samples, 2 * samples), jnp.bfloat16),
            jax.ShapeDtypeStruct((orients, 4 * cols, 4 * cols), jnp.bfloat16),
            jax.ShapeDtypeStruct((orients, 2 * rows, 2 * window), jnp.bfloat16),
            jax.ShapeDtypeStruct(traces.shape, traces.dtype),
        ),
        in_specs=[pl.BlockSpec(memory_space=pltpu.SMEM), vmem],
        out_specs=(vmem, vmem, vmem, vmem),
        compiler_params=pltpu.CompilerParams(vmem_limit_bytes=8 * 2**20),
        name="filter_matrices",
        cost_estimate=pl.CostEstimate(flops=0, bytes_accessed=4_000_000, transcendentals=0),
    )(directions, traces)

    swap_one, swap_two, time_mats, xline_mats, inline_mats, own = lax.optimization_barrier(
        (swap_one, swap_two, time_mats, xline_mats, inline_mats, own)
    )
    swap_one_other = exchange(swap_one, "xline", core_pairs)
    swap_two_other = exchange(swap_two, "xline", core_pairs)

    spread_out = lambda values, fill: jnp.pad(
        values, ((0, 0), (0, LANES - values.shape[1])), constant_values=fill
    )
    params = jnp.concatenate(
        [
            spread_out(init_means, 0.0),
            spread_out(init_variances, 1.0),
            jnp.broadcast_to(init_weights[:, None], (components, LANES)),
        ],
        axis=0,
    )
    whole = lambda *shape: pl.BlockSpec(shape, lambda o: (0,) * len(shape))
    chunk = 6
    unit = 2 if rows % 2 == 0 else 1
    features, sums = pl.pallas_call(
        functools.partial(
            features_kernel, (orients, samples, cols, rows, window, components, chunk, unit)
        ),
        grid=(orients // 2,),
        out_shape=(
            jax.ShapeDtypeStruct((rows * cols * (slot + 1), samples), jnp.float32),
            jax.ShapeDtypeStruct((components, LANES), jnp.float32),
        ),
        in_specs=[whole(rows, cols, samples)] * 6
        + [
            pl.BlockSpec((2, samples, 2 * samples), lambda o: (o, 0, 0)),
            pl.BlockSpec((2, 4 * cols, 4 * cols), lambda o: (o, 0, 0)),
            whole(orients, 2 * rows, 2 * window),
            whole(3 * components, LANES),
        ],
        out_specs=(whole(rows * cols * (slot + 1), samples), whole(components, LANES)),
        scratch_shapes=[
            pltpu.VMEM((window * 2 * cols, samples), jnp.bfloat16),
            pltpu.VMEM((4 * cols * (window + 1), samples), jnp.float32),
            pltpu.VMEM((4 * cols * (window + 1), samples), jnp.float32),
            pltpu.VMEM((4 * slot, 2 * components), jnp.float32),
            pltpu.VMEM((4 * slot, unit * cols * samples), jnp.bfloat16),
            pltpu.VMEM((components, unit * cols * samples), jnp.float32),
        ],
        compiler_params=pltpu.CompilerParams(vmem_limit_bytes=40 * 2**20),
        name="features_and_first_moments",
    )(
        own, other, swap_one, swap_one_other, swap_two, swap_two_other,
        time_mats, xline_mats, inline_mats,
        params,
    )
    sums = group_sum(sums)
    cells = inlines * rows * lax.axis_size("xline") * cols * samples
    posterior, sums, centers, spreads = pl.pallas_call(
        functools.partial(
            posterior_kernel, (orients, samples, cols, rows, components, chunk, unit, cells)
        ),
        grid=(rows // unit + 1,),
        out_shape=(
            jax.ShapeDtypeStruct((rows, components, cols, samples), jnp.bfloat16),
            jax.ShapeDtypeStruct((components, LANES), jnp.float32),
            jax.ShapeDtypeStruct((components, LANES), jnp.float32),
            jax.ShapeDtypeStruct((components, LANES), jnp.float32),
        ),
        in_specs=[
            whole(rows * cols * (slot + 1), samples),
            whole(3 * components, LANES),
            whole(components, LANES),
        ],
        out_specs=(
            pl.BlockSpec((unit, components, cols, samples), lambda r: (jnp.maximum(r - 1, 0), 0, 0, 0)),
            whole(components, LANES),
            whole(components, LANES),
            whole(components, LANES),
        ),
        scratch_shapes=[
            pltpu.VMEM((2 * components, 6 * slot), jnp.bfloat16),
            pltpu.VMEM((4 * slot, 2 * components), jnp.float32),
            pltpu.VMEM((unit, components * (cols + 1), samples), jnp.float32),
            pltpu.VMEM((4 * slot, unit * cols * samples), jnp.bfloat16),
            pltpu.VMEM((components, unit * cols * samples), jnp.float32),
        ],
        compiler_params=pltpu.CompilerParams(vmem_limit_bytes=40 * 2**20),
        name="posterior_and_second_moments",
    )(features, params, sums)
    sums = group_sum(sums)
    means, variances, weights = pl.pallas_call(
        functools.partial(update_kernel, (feats, slot, cells)),
        out_shape=(
            jax.ShapeDtypeStruct((feats, components), jnp.float32),
            jax.ShapeDtypeStruct((feats, components), jnp.float32),
            jax.ShapeDtypeStruct((1, components), jnp.float32),
        ),
        in_specs=[vmem, vmem, vmem],
        out_specs=(vmem, vmem, vmem),
        compiler_params=pltpu.CompilerParams(vmem_limit_bytes=8 * 2**20),
        name="last_update",
    )(sums, centers, spreads)
    return posterior, means.T, variances.T, weights.reshape(components)


def solution(mesh):
    in_specs = (P(("slab", "inline"), "xline", None), P(), P(), P(), P())
    out_specs = (
        P(("slab", "inline"), None, "xline", None),
        P("slab", None),
        P("slab", None),
        P("slab"),
    )
    return jax.shard_map(
        per_device, mesh=mesh, in_specs=in_specs, out_specs=out_specs, check_vma=False
    )
```

```python
import functools
import math

import jax
import jax.numpy as jnp
from jax import lax
from jax.experimental import pallas as pl
from jax.experimental.pallas import tpu as pltpu
from jax.sharding import PartitionSpec as P

TAPS = 31
HALF = 15
AZIMUTHS = 8
DIPS = 4
LANES = 128
SUBLANES = 8

eps_mag = 0.01
wavenumber = math.pi / 4.0


def round_up(value, step):
    return (value + step - 1) // step * step


def split(values, count):
    pieces = []
    for _ in range(count):
        pieces.append(values.astype(jnp.bfloat16))
        values = values - pieces[-1].astype(jnp.float32)
    return pieces


def tap_lines(directions_ref, orients):
    shape = (round_up(orients, SUBLANES), LANES)
    rows = lax.broadcasted_iota(jnp.int32, shape, 0)
    lanes = lax.broadcasted_iota(jnp.int32, shape, 1)
    direction = jnp.zeros(shape, jnp.int32)
    for orient in range(orients):
        direction = jnp.where(rows == orient, directions_ref[orient], direction)
    azimuth = lax.rem(direction, AZIMUTHS).astype(jnp.float32) * (math.pi / AZIMUTHS)
    dip_angle = (lax.div(direction, AZIMUTHS) + 1).astype(jnp.float32) * (math.pi / (2 * DIPS + 2))
    offsets = lanes.astype(jnp.float32) - HALF
    used = lanes < TAPS
    width_scale = HALF / 3.0
    envelope = jnp.exp(-offsets * offsets / (2.0 * width_scale * width_scale))
    envelope = jnp.where(used, envelope, 0.0)
    envelope = envelope / jnp.sqrt(jnp.sum(envelope * envelope, axis=1, keepdims=True))
    sine = jnp.sin(dip_angle)
    lines = []
    for wave, sign in (
        (wavenumber * (sine * jnp.cos(azimuth)), 1.0),
        (wavenumber * (sine * jnp.sin(azimuth)), 1.0),
        (wavenumber * jnp.cos(dip_angle), -1.0),
    ):
        phase = wave * (offsets * sign)
        pair = (envelope * jnp.cos(phase), envelope * jnp.sin(phase))
        lines.append([part.astype(jnp.bfloat16).astype(jnp.float32) for part in pair])
    return lines


def matrices_kernel(dims, directions_ref, own_ref, time_ref, xline_ref, inline_ref, kept_ref):
    orients, samples, cols, rows, window = dims
    side = lax.axis_index("xline")
    lanes = lax.broadcasted_iota(jnp.int32, (SUBLANES, LANES), 1)[:1]
    lines = tap_lines(directions_ref, orients)
    kept_ref[...] = own_ref[...]

    def sheared(line, count, shift, width):
        if width > LANES:
            line = jnp.concatenate([line, jnp.zeros((1, width - LANES), jnp.float32)], axis=1)
        wide = jnp.broadcast_to(line, (count, width))
        return pltpu.roll(wide, shift % width, 1, stride=1, stride_axis=0)

    for orient in range(orients):
        line = lambda axis, part: lines[axis][part][orient : orient + 1]
        for part in range(2):
            time_ref[orient, :, part * samples : (part + 1) * samples] = sheared(
                line(2, part), samples, 2 * samples - HALF, 2 * samples
            )[:, :samples].astype(jnp.bfloat16)

        def xline_half(part, half, slot):
            shift = LANES - HALF + slot * cols
            if half:
                moved = jnp.where(
                    side == 0,
                    sheared(line(1, part), cols, shift + LANES - cols, LANES),
                    sheared(line(1, part), cols, shift + cols, LANES),
                )
            else:
                moved = sheared(line(1, part), cols, shift, LANES)
            return jnp.where((lanes >= slot * cols) & (lanes < (slot + 1) * cols), moved, 0.0)

        cosine = [xline_half(0, 0, p * 2) + xline_half(0, 1, p * 2 + 1) for p in range(2)]
        sine = [xline_half(1, 0, p * 2) + xline_half(1, 1, p * 2 + 1) for p in range(2)]
        xline_ref[orient] = jnp.concatenate(
            [
                cosine[0] - sine[1],
                sine[0] + cosine[1],
                cosine[0] + sine[1],
                sine[0] - cosine[1],
            ],
            axis=0,
        )[:, : 4 * cols].astype(jnp.bfloat16)

        def inline_part(part, slot):
            moved = sheared(line(0, part), rows, slot * window, LANES)
            return jnp.where((lanes >= slot * window) & (lanes < (slot + 1) * window), moved, 0.0)

        inline_ref[orient] = jnp.concatenate(
            [
                inline_part(0, 0) - inline_part(1, 1),
                inline_part(1, 0) + inline_part(0, 1),
            ],
            axis=0,
        )[:, : 2 * window].astype(jnp.bfloat16)


def score_matrix(centers, spreads, log_weights, feats, slot, levels):
    lanes = lax.broadcasted_iota(jnp.int32, centers.shape, 1)
    real = lanes < feats
    inverse = 1.0 / spreads
    widen = lambda values, count: [p.astype(jnp.float32) for p in split(values, count)]
    linear = widen(centers * inverse, levels)
    square = widen(-0.5 * inverse, levels)
    kept_linear, kept_square = sum(linear), sum(square)
    terms = jnp.log(2.0 * math.pi * spreads) - 0.5 * kept_linear * (kept_linear / kept_square)
    constant = log_weights - 0.5 * jnp.sum(jnp.where(real, terms, 0.0), axis=1, keepdims=True)
    constants = widen(constant, 3)
    groups = []
    for level in range(levels):
        first = jnp.where(real, linear[level], 0.0)
        first = jnp.where(lanes == feats, constants[level], first)
        if level == 0 and levels == 2:
            first = jnp.where(lanes == feats + 1, constants[2], first)
        both = first + pltpu.roll(jnp.where(real, square[level], 0.0), slot, 1)
        both = jnp.concatenate([both, jnp.zeros_like(both)], axis=1)
        groups.append(both + pltpu.roll(both, 2 * slot, 1) + pltpu.roll(both, 4 * slot, 1))
    return jnp.concatenate(groups, axis=0)[:, : 6 * slot].astype(jnp.bfloat16)


def split_features(features):
    both = jnp.concatenate([features, features * features], axis=0)
    return jnp.concatenate(split(both, 3), axis=0)


def score_stage(data, matrix, scores_ref, place, components):
    scores = jnp.dot(matrix, data, preferred_element_type=jnp.float32)
    scores_ref[:, place] = sum(
        scores[k : k + components] for k in range(0, matrix.shape[0], components)
    )


def moment_stage(data, scores_ref, place):
    scores = scores_ref[:, place]
    exponent = jnp.exp(scores - jnp.max(scores, axis=0, keepdims=True))
    shares = exponent * (1.0 / jnp.sum(exponent, axis=0, keepdims=True))
    high = shares.astype(jnp.bfloat16)
    low = (shares - high.astype(jnp.float32)).astype(jnp.bfloat16)
    sums = lax.dot_general(
        data,
        jnp.concatenate([high, low], axis=0),
        (((1,), (1,)), ((), ())),
        preferred_element_type=jnp.float32,
    )
    return shares, sums


def gathered(features_ref, row, rows, first, count, slot):
    place = lambda col: (col * rows + row) * (slot + 1)
    return jnp.concatenate(
        [features_ref[pl.ds(place(first + k), slot), :] for k in range(count)], axis=1
    )


def fold_sums(total, components, slot):
    both = total[:, :components] + total[:, components:]
    both = both[: 2 * slot] + both[2 * slot :]
    return jnp.concatenate(
        [both, jnp.zeros((LANES - 2 * slot, components), jnp.float32)], axis=0
    ).T


def features_kernel(dims, *refs):
    orients, samples, cols, rows, window, components, chunk, unit = dims
    halves, refs = refs[:6], refs[6:]
    time_ref, xline_ref, inline_ref, params_ref = refs[:4]
    split_ref, sums_ref, features_ref, traces, across_even, across_odd, total, data, scores = refs[4:]
    feats = 2 * orients
    slot = round_up(feats + 2, SUBLANES)
    twice = pl.program_id(0)
    @pl.when(twice == 0)
    def _():
        own, other, swap_one, swap_one_other, swap_two, swap_two_other = halves
        even = lax.rem(lax.axis_index("inline"), 2) == 0

        def put(place, near, far):
            traces[pl.ds(place * 2 * cols, 2 * cols), :] = jnp.concatenate(
                [near.astype(jnp.float32), far.astype(jnp.float32)], axis=0
            ).astype(jnp.bfloat16)

        for row in range(rows):
            put(HALF + row, own[row], other[row])
            one = swap_one[row].astype(jnp.float32)
            one_far = swap_one_other[row].astype(jnp.float32)
            two = swap_two[row].astype(jnp.float32)
            two_far = swap_two_other[row].astype(jnp.float32)
            if row >= rows - HALF:
                put(row - (rows - HALF), jnp.where(even, two, one), jnp.where(even, two_far, one_far))
            if row < HALF:
                put(HALF + rows + row, jnp.where(even, one, two), jnp.where(even, one_far, two_far))
        for place in range(rows + 2 * HALF, window):
            traces[pl.ds(place * 2 * cols, 2 * cols), :] = jnp.zeros(
                (2 * cols, samples), jnp.bfloat16
            )
        for extra in range(feats, slot):
            filler = jnp.full((rows, samples), 1.0 if extra < feats + 2 else 0.0, jnp.float32)
            for col in range(cols):
                place = col * rows * (slot + 1) + extra
                features_ref[pl.ds(place, rows, stride=slot + 1), :] = filler

    lines = 2 * cols
    apart = window + 1

    def magnitudes(orient, across, piece):
        polarity, col = piece // (cols // 2), piece % (cols // 2) * 2

        def taken(k, part):
            place = ((polarity * 2 + part) * cols + col + k) * apart
            return across[pl.ds(place, window), :]

        stacked = jnp.concatenate(
            [jnp.concatenate([taken(k, 0), taken(k, 1)], axis=0) for k in range(2)], axis=1
        ).astype(jnp.bfloat16)
        found = jnp.dot(inline_ref[orient], stacked, preferred_element_type=jnp.float32)
        real_part, imag_part = found[:rows], found[rows:]
        power = real_part * real_part + imag_part * imag_part + eps_mag
        size = power * lax.rsqrt(power)
        for k in range(2):
            place = (col + k) * rows * (slot + 1) + 2 * orient + polarity
            features_ref[pl.ds(place, rows, stride=slot + 1), :] = size[
                :, k * samples : (k + 1) * samples
            ]

    def filtered(which, across, before, across_before):
        band = jnp.dot(traces[...], time_ref[which], preferred_element_type=jnp.float32)
        band = band.astype(jnp.bfloat16)
        done = 0
        for pair in range(window // 2):

            def piece(k, p):
                first = (pair * 2 + k) * lines
                return band[first : first + lines, p * samples : (p + 1) * samples]

            stacked = jnp.concatenate(
                [jnp.concatenate([piece(k, 0), piece(k, 1)], axis=0) for k in range(2)], axis=1
            )
            crossed = jnp.dot(xline_ref[which], stacked, preferred_element_type=jnp.float32)
            for k in range(2):
                across[pl.ds(2 * pair + k, 4 * cols, stride=apart), :] = crossed[
                    :, k * samples : (k + 1) * samples
                ]
            until = cols * (pair + 1) // (window // 2)
            for other in range(done, until):
                magnitudes(before, across_before, other)
            done = until

    filtered(0, across_even, jnp.maximum(2 * twice - 1, 0), across_odd)
    filtered(1, across_odd, 2 * twice, across_even)

    @pl.when(twice == orients // 2 - 1)
    def _():
        for piece in range(cols):
            magnitudes(orients - 1, across_odd, piece)

    @pl.when(twice == orients // 2 - 1)
    def _():
        matrix = score_matrix(
            params_ref[:components],
            params_ref[components : 2 * components],
            jnp.log(params_ref[2 * components :, :1]),
            feats, slot, 3,
        )
        total[...] = jnp.zeros(total.shape, jnp.float32)


        def sweep(block, moments, scoring):
            partial = jnp.zeros(total.shape, jnp.float32)
            for start in range(0, unit * cols, chunk):
                place = slice(start * samples, (start + chunk) * samples)
                if moments:
                    partial = partial + moment_stage(data[:, place], scores, place)[1]
                if scoring:
                    row = block * unit + start // cols
                    lines = gathered(features_ref, row, rows, start % cols, chunk, slot)
                    pieces = split_features(lines)
                    data[:, place] = pieces[: data.shape[0]]
                    split_ref[block, :, place] = pieces
                    score_stage(pieces, matrix, scores, place, components)
            if moments:
                total[...] += partial

        sweep(0, False, True)

        @pl.loop(1, rows // unit)
        def _(block):
            sweep(block, True, True)

        sweep(0, True, False)
        sums_ref[...] = fold_sums(total[...], components, slot)


def new_params(sums, centers, spreads, feats, slot, cells):
    components = centers.shape[0]
    mass = sums[:, feats : feats + 1]
    first = sums
    second = pltpu.roll(sums, LANES - slot, 1)
    scale = 1.0 / (mass + 1.0)
    moved = (first + centers) * scale
    centred = second - 2.0 * moved * first + moved * moved * mass
    return moved, (centred + spreads) * scale, (mass + 1.0) / (cells + components)


def posterior_kernel(dims, *refs):
    orients, samples, cols, rows, components, chunk, unit, cells = dims
    split_ref, params_ref, before_ref = refs[:3]
    posterior_ref, sums_ref, centers_ref, spreads_ref, matrix, total, turned, scores = refs[3:]
    feats = 2 * orients
    slot = round_up(feats + 2, SUBLANES)
    step = pl.program_id(0)

    @pl.when(step == 0)
    def _():
        centers, spreads, weights = new_params(
            before_ref[...],
            params_ref[:components],
            params_ref[components : 2 * components],
            feats, slot, cells,
        )
        lanes = lax.broadcasted_iota(jnp.int32, centers.shape, 1)
        centers = jnp.where(lanes < feats, centers, 0.0)
        spreads = jnp.where(lanes < feats, spreads, 1.0)
        centers_ref[...] = centers
        spreads_ref[...] = spreads
        matrix[...] = score_matrix(centers, spreads, jnp.log(weights), feats, slot, 2)
        total[...] = jnp.zeros(total.shape, jnp.float32)

    def sweep(moments, scoring):
        partial = jnp.zeros(total.shape, jnp.float32)
        for start in range(0, unit * cols, chunk):
            place = slice(start * samples, (start + chunk) * samples)
            which, col = start // cols, start % cols
            if moments:
                before = split_ref[step - 1, : 4 * slot, place]
                shares, sums = moment_stage(before, scores, place)
            if scoring:
                score_stage(split_ref[step, :, place], matrix[...], scores, place, components)
            if moments:
                partial = partial + sums
                for k in range(chunk):
                    turned[which, pl.ds(col + k, components, stride=cols + 1), :] = shares[
                        :, k * samples : (k + 1) * samples
                    ]
        if moments:
            total[...] += partial
            for which in range(unit):
                for component in range(components):
                    posterior_ref[which, component] = turned[
                        which, pl.ds(component * (cols + 1), cols), :
                    ].astype(jnp.bfloat16)

    last = rows // unit
    pl.when(step == 0)(lambda: sweep(False, True))
    pl.when((step > 0) & (step < last))(lambda: sweep(True, True))
    pl.when(step == last)(lambda: sweep(True, False))

    @pl.when(step == pl.num_programs(0) - 1)
    def _():
        sums_ref[...] = fold_sums(total[...], components, slot)


def update_kernel(dims, sums_ref, centers_ref, spreads_ref, means_ref, variances_ref, weights_ref):
    feats, slot, cells = dims
    components = sums_ref.shape[0]
    rest = jnp.zeros((LANES - 3 * components, LANES), jnp.float32)
    turned = jnp.concatenate(
        [sums_ref[...], centers_ref[...], spreads_ref[...], rest], axis=0
    ).T
    part = lambda first, group: turned[
        first : first + feats, group * components : (group + 1) * components
    ]
    mass = turned[feats : feats + 1, :components]
    first, second, centers, spreads = part(0, 0), part(slot, 0), part(0, 1), part(0, 2)
    moved = (first + centers) / (mass + 1.0)
    centred = second - 2.0 * moved * first + moved * moved * mass
    means_ref[...] = moved
    variances_ref[...] = (centred + spreads) / (mass + 1.0)
    weights_ref[...] = (mass + 1.0) / (cells + components)


def exchange(values, axis, pairs):
    return lax.ppermute(values, axis, [p for a, b in pairs for p in ((a, b), (b, a))])


def group_sum(values):
    axes = ("inline", "xline")
    count = lax.axis_size("inline") * lax.axis_size("xline")
    if count & (count - 1):
        return lax.psum(values, axes)
    rounds = []
    while count > 1:
        rounds.append(min(4, count))
        count //= rounds[-1]
    for radix in rounds:
        count *= radix
    step = count
    for radix in rounds:
        step //= radix
        arrived = [
            lax.ppermute(values, axes, [(i, i ^ (step * d)) for i in range(count)])
            for d in range(1, radix)
        ]
        if radix == 4:
            values = (values + arrived[0]) + (arrived[1] + arrived[2])
        else:
            values = values + arrived[0]
    return values


def per_device(traces, directions, init_means, init_variances, init_weights):
    rows, cols, samples = traces.shape
    orients = directions.shape[0]
    components = init_weights.shape[0]
    feats = 2 * orients
    slot = round_up(feats + 2, SUBLANES)
    window = round_up(rows + 2 * HALF, 16)
    inlines = lax.axis_size("inline")
    if lax.axis_size("xline") != 2 or samples != LANES or rows < HALF or orients % 2 or cols % 2:
        raise ValueError("unsupported sizes")

    core_pairs = [(0, 1)]
    other = exchange(traces, "xline", core_pairs)
    swap_one = exchange(traces, "inline", [(i, i + 1) for i in range(0, inlines - 1, 2)])
    swap_two = exchange(traces, "inline", [(i, i + 1) for i in range(1, inlines - 1, 2)])
    vmem = pl.BlockSpec(memory_space=pltpu.VMEM)
    time_mats, xline_mats, inline_mats, own = pl.pallas_call(
        functools.partial(matrices_kernel, (orients, samples, cols, rows, window)),
        out_shape=(
            jax.ShapeDtypeStruct((orients, samples, 2 * samples), jnp.bfloat16),
            jax.ShapeDtypeStruct((orients, 4 * cols, 4 * cols), jnp.bfloat16),
            jax.ShapeDtypeStruct((orients, 2 * rows, 2 * window), jnp.bfloat16),
            jax.ShapeDtypeStruct(traces.shape, traces.dtype),
        ),
        in_specs=[pl.BlockSpec(memory_space=pltpu.SMEM), vmem],
        out_specs=(vmem, vmem, vmem, vmem),
        compiler_params=pltpu.CompilerParams(vmem_limit_bytes=8 * 2**20),
        name="filter_matrices",
        cost_estimate=pl.CostEstimate(flops=0, bytes_accessed=4_000_000, transcendentals=0),
    )(directions, traces)

    swap_one, swap_two, time_mats, xline_mats, inline_mats, own = lax.optimization_barrier(
        (swap_one, swap_two, time_mats, xline_mats, inline_mats, own)
    )
    swap_one_other = exchange(swap_one, "xline", core_pairs)
    swap_two_other = exchange(swap_two, "xline", core_pairs)

    spread_out = lambda values, fill: jnp.pad(
        values, ((0, 0), (0, LANES - values.shape[1])), constant_values=fill
    )
    params = jnp.concatenate(
        [
            spread_out(init_means, 0.0),
            spread_out(init_variances, 1.0),
            jnp.broadcast_to(init_weights[:, None], (components, LANES)),
        ],
        axis=0,
    )
    whole = lambda *shape: pl.BlockSpec(shape, lambda o: (0,) * len(shape))
    chunk = 6
    unit = 2 if rows % 2 == 0 else 1
    split_shape = (rows // unit, 6 * slot, unit * cols * samples)
    pieces, sums = pl.pallas_call(
        functools.partial(
            features_kernel, (orients, samples, cols, rows, window, components, chunk, unit)
        ),
        grid=(orients // 2,),
        out_shape=(
            jax.ShapeDtypeStruct(split_shape, jnp.bfloat16),
            jax.ShapeDtypeStruct((components, LANES), jnp.float32),
        ),
        in_specs=[whole(rows, cols, samples)] * 6
        + [
            pl.BlockSpec((2, samples, 2 * samples), lambda o: (o, 0, 0)),
            pl.BlockSpec((2, 4 * cols, 4 * cols), lambda o: (o, 0, 0)),
            whole(orients, 2 * rows, 2 * window),
            whole(3 * components, LANES),
        ],
        out_specs=(whole(*split_shape), whole(components, LANES)),
        scratch_shapes=[
            pltpu.VMEM((rows * cols * (slot + 1), samples), jnp.float32),
            pltpu.VMEM((window * 2 * cols, samples), jnp.bfloat16),
            pltpu.VMEM((4 * cols * (window + 1), samples), jnp.float32),
            pltpu.VMEM((4 * cols * (window + 1), samples), jnp.float32),
            pltpu.VMEM((4 * slot, 2 * components), jnp.float32),
            pltpu.VMEM((4 * slot, unit * cols * samples), jnp.bfloat16),
            pltpu.VMEM((components, unit * cols * samples), jnp.float32),
        ],
        compiler_params=pltpu.CompilerParams(vmem_limit_bytes=28 * 2**20),
        name="features_and_first_moments",
    )(
        own, other, swap_one, swap_one_other, swap_two, swap_two_other,
        time_mats, xline_mats, inline_mats,
        params,
    )
    sums = group_sum(sums)
    cells = inlines * rows * lax.axis_size("xline") * cols * samples
    posterior, sums, centers, spreads = pl.pallas_call(
        functools.partial(
            posterior_kernel, (orients, samples, cols, rows, components, chunk, unit, cells)
        ),
        grid=(rows // unit + 1,),
        out_shape=(
            jax.ShapeDtypeStruct((rows, components, cols, samples), jnp.bfloat16),
            jax.ShapeDtypeStruct((components, LANES), jnp.float32),
            jax.ShapeDtypeStruct((components, LANES), jnp.float32),
            jax.ShapeDtypeStruct((components, LANES), jnp.float32),
        ),
        in_specs=[
            whole(*split_shape),
            whole(3 * components, LANES),
            whole(components, LANES),
        ],
        out_specs=(
            pl.BlockSpec((unit, components, cols, samples), lambda r: (jnp.maximum(r - 1, 0), 0, 0, 0)),
            whole(components, LANES),
            whole(components, LANES),
            whole(components, LANES),
        ),
        scratch_shapes=[
            pltpu.VMEM((2 * components, 6 * slot), jnp.bfloat16),
            pltpu.VMEM((4 * slot, 2 * components), jnp.float32),
            pltpu.VMEM((unit, components * (cols + 1), samples), jnp.float32),
            pltpu.VMEM((components, unit * cols * samples), jnp.float32),
        ],
        compiler_params=pltpu.CompilerParams(vmem_limit_bytes=28 * 2**20),
        name="posterior_and_second_moments",
    )(pieces, params, sums)
    sums = group_sum(sums)
    means, variances, weights = pl.pallas_call(
        functools.partial(update_kernel, (feats, slot, cells)),
        out_shape=(
            jax.ShapeDtypeStruct((feats, components), jnp.float32),
            jax.ShapeDtypeStruct((feats, components), jnp.float32),
            jax.ShapeDtypeStruct((1, components), jnp.float32),
        ),
        in_specs=[vmem, vmem, vmem],
        out_specs=(vmem, vmem, vmem),
        compiler_params=pltpu.CompilerParams(vmem_limit_bytes=8 * 2**20),
        name="last_update",
    )(sums, centers, spreads)
    return posterior, means.T, variances.T, weights.reshape(components)


def solution(mesh):
    in_specs = (P(("slab", "inline"), "xline", None), P(), P(), P(), P())
    out_specs = (
        P(("slab", "inline"), None, "xline", None),
        P("slab", None),
        P("slab", None),
        P("slab"),
    )
    return jax.shard_map(
        per_device, mesh=mesh, in_specs=in_specs, out_specs=out_specs, check_vma=False
    )
```

```python
import functools
import math

import jax
import jax.numpy as jnp
from jax import lax
from jax.experimental import pallas as pl
from jax.experimental.pallas import tpu as pltpu
from jax.sharding import PartitionSpec as P

TAPS = 31
HALF = 15
AZIMUTHS = 8
DIPS = 4
LANES = 128
SUBLANES = 8

eps_mag = 0.01
wavenumber = math.pi / 4.0


def round_up(value, step):
    return (value + step - 1) // step * step


def split(values, count):
    pieces = []
    for _ in range(count):
        pieces.append(values.astype(jnp.bfloat16))
        values = values - pieces[-1].astype(jnp.float32)
    return pieces


def tap_lines(directions_ref, orients):
    shape = (round_up(orients, SUBLANES), LANES)
    rows = lax.broadcasted_iota(jnp.int32, shape, 0)
    lanes = lax.broadcasted_iota(jnp.int32, shape, 1)
    direction = jnp.zeros(shape, jnp.int32)
    for orient in range(orients):
        direction = jnp.where(rows == orient, directions_ref[orient], direction)
    azimuth = lax.rem(direction, AZIMUTHS).astype(jnp.float32) * (math.pi / AZIMUTHS)
    dip_angle = (lax.div(direction, AZIMUTHS) + 1).astype(jnp.float32) * (math.pi / (2 * DIPS + 2))
    offsets = lanes.astype(jnp.float32) - HALF
    used = lanes < TAPS
    width_scale = HALF / 3.0
    envelope = jnp.exp(-offsets * offsets / (2.0 * width_scale * width_scale))
    envelope = jnp.where(used, envelope, 0.0)
    envelope = envelope / jnp.sqrt(jnp.sum(envelope * envelope, axis=1, keepdims=True))
    sine = jnp.sin(dip_angle)
    lines = []
    for wave, sign in (
        (wavenumber * (sine * jnp.cos(azimuth)), 1.0),
        (wavenumber * (sine * jnp.sin(azimuth)), 1.0),
        (wavenumber * jnp.cos(dip_angle), -1.0),
    ):
        phase = wave * (offsets * sign)
        pair = (envelope * jnp.cos(phase), envelope * jnp.sin(phase))
        lines.append([part.astype(jnp.bfloat16).astype(jnp.float32) for part in pair])
    return lines


def matrices_kernel(dims, directions_ref, own_ref, time_ref, xline_ref, inline_ref, kept_ref):
    orients, samples, cols, rows, window = dims
    side = lax.axis_index("xline")
    lanes = lax.broadcasted_iota(jnp.int32, (SUBLANES, LANES), 1)[:1]
    lines = tap_lines(directions_ref, orients)
    kept_ref[...] = own_ref[...]

    def sheared(line, count, shift, width):
        if width > LANES:
            line = jnp.concatenate([line, jnp.zeros((1, width - LANES), jnp.float32)], axis=1)
        wide = jnp.broadcast_to(line, (count, width))
        return pltpu.roll(wide, shift % width, 1, stride=1, stride_axis=0)

    for orient in range(orients):
        line = lambda axis, part: lines[axis][part][orient : orient + 1]
        for part in range(2):
            time_ref[orient, :, part * samples : (part + 1) * samples] = sheared(
                line(2, part), samples, 2 * samples - HALF, 2 * samples
            )[:, :samples].astype(jnp.bfloat16)

        def xline_half(part, half, slot):
            shift = LANES - HALF + slot * cols
            if half:
                moved = jnp.where(
                    side == 0,
                    sheared(line(1, part), cols, shift + LANES - cols, LANES),
                    sheared(line(1, part), cols, shift + cols, LANES),
                )
            else:
                moved = sheared(line(1, part), cols, shift, LANES)
            return jnp.where((lanes >= slot * cols) & (lanes < (slot + 1) * cols), moved, 0.0)

        cosine = [xline_half(0, 0, p * 2) + xline_half(0, 1, p * 2 + 1) for p in range(2)]
        sine = [xline_half(1, 0, p * 2) + xline_half(1, 1, p * 2 + 1) for p in range(2)]
        xline_ref[orient] = jnp.concatenate(
            [
                cosine[0] - sine[1],
                sine[0] + cosine[1],
                cosine[0] + sine[1],
                sine[0] - cosine[1],
            ],
            axis=0,
        )[:, : 4 * cols].astype(jnp.bfloat16)

        def inline_part(part, slot):
            moved = sheared(line(0, part), rows, slot * window, LANES)
            return jnp.where((lanes >= slot * window) & (lanes < (slot + 1) * window), moved, 0.0)

        inline_ref[orient] = jnp.concatenate(
            [
                inline_part(0, 0) - inline_part(1, 1),
                inline_part(1, 0) + inline_part(0, 1),
            ],
            axis=0,
        )[:, : 2 * window].astype(jnp.bfloat16)


def score_matrix(centers, spreads, log_weights, feats, slot, levels):
    lanes = lax.broadcasted_iota(jnp.int32, centers.shape, 1)
    real = lanes < feats
    inverse = 1.0 / spreads
    widen = lambda values, count: [p.astype(jnp.float32) for p in split(values, count)]
    linear = widen(centers * inverse, levels)
    square = widen(-0.5 * inverse, levels)
    kept_linear, kept_square = sum(linear), sum(square)
    terms = jnp.log(2.0 * math.pi * spreads) - 0.5 * kept_linear * (kept_linear / kept_square)
    constant = log_weights - 0.5 * jnp.sum(jnp.where(real, terms, 0.0), axis=1, keepdims=True)
    constants = widen(constant, 3)
    groups = []
    for level in range(levels):
        first = jnp.where(real, linear[level], 0.0)
        first = jnp.where(lanes == feats, constants[level], first)
        if level == 0 and levels == 2:
            first = jnp.where(lanes == feats + 1, constants[2], first)
        both = first + pltpu.roll(jnp.where(real, square[level], 0.0), slot, 1)
        both = jnp.concatenate([both, jnp.zeros_like(both)], axis=1)
        groups.append(both + pltpu.roll(both, 2 * slot, 1) + pltpu.roll(both, 4 * slot, 1))
    return jnp.concatenate(groups, axis=0)[:, : 6 * slot].astype(jnp.bfloat16)


def split_features(features):
    both = jnp.concatenate([features, features * features], axis=0)
    return jnp.concatenate(split(both, 3), axis=0)


def score_stage(data, matrix, scores_ref, place, components):
    scores = jnp.dot(matrix, data, preferred_element_type=jnp.float32)
    scores_ref[:, place] = sum(
        scores[k : k + components] for k in range(0, matrix.shape[0], components)
    )


def moment_stage(data, scores_ref, place):
    scores = scores_ref[:, place]
    exponent = jnp.exp(scores - jnp.max(scores, axis=0, keepdims=True))
    shares = exponent * (1.0 / jnp.sum(exponent, axis=0, keepdims=True))
    high = shares.astype(jnp.bfloat16)
    low = (shares - high.astype(jnp.float32)).astype(jnp.bfloat16)
    sums = lax.dot_general(
        data,
        jnp.concatenate([high, low], axis=0),
        (((1,), (1,)), ((), ())),
        preferred_element_type=jnp.float32,
    )
    return shares, sums


def gathered(features_ref, row, rows, first, count, slot):
    place = lambda col: (col * rows + row) * (slot + 1)
    return jnp.concatenate(
        [features_ref[pl.ds(place(first + k), slot), :] for k in range(count)], axis=1
    )


def fold_sums(total, components, slot):
    both = total[:, :components] + total[:, components:]
    both = both[: 2 * slot] + both[2 * slot :]
    return jnp.concatenate(
        [both, jnp.zeros((LANES - 2 * slot, components), jnp.float32)], axis=0
    ).T


def features_kernel(dims, *refs):
    orients, samples, cols, rows, window, components, chunk, unit = dims
    halves, refs = refs[:6], refs[6:]
    time_ref, xline_ref, inline_ref, params_ref = refs[:4]
    split_ref, sums_ref, features_ref, traces, across_even, across_odd, total, data, scores = refs[4:]
    feats = 2 * orients
    slot = round_up(feats + 2, SUBLANES)
    twice = pl.program_id(0)
    @pl.when(twice == 0)
    def _():
        own, other, swap_one, swap_one_other, swap_two, swap_two_other = halves
        even = lax.rem(lax.axis_index("inline"), 2) == 0

        def put(place, near, far):
            traces[pl.ds(place * 2 * cols, 2 * cols), :] = jnp.concatenate(
                [near.astype(jnp.float32), far.astype(jnp.float32)], axis=0
            ).astype(jnp.bfloat16)

        for row in range(rows):
            put(HALF + row, own[row], other[row])
            one = swap_one[row].astype(jnp.float32)
            one_far = swap_one_other[row].astype(jnp.float32)
            two = swap_two[row].astype(jnp.float32)
            two_far = swap_two_other[row].astype(jnp.float32)
            if row >= rows - HALF:
                put(row - (rows - HALF), jnp.where(even, two, one), jnp.where(even, two_far, one_far))
            if row < HALF:
                put(HALF + rows + row, jnp.where(even, one, two), jnp.where(even, one_far, two_far))
        for place in range(rows + 2 * HALF, window):
            traces[pl.ds(place * 2 * cols, 2 * cols), :] = jnp.zeros(
                (2 * cols, samples), jnp.bfloat16
            )
        for extra in range(feats, slot):
            filler = jnp.full((rows, samples), 1.0 if extra < feats + 2 else 0.0, jnp.float32)
            for col in range(cols):
                place = col * rows * (slot + 1) + extra
                features_ref[pl.ds(place, rows, stride=slot + 1), :] = filler

    lines = 2 * cols
    apart = window + 1

    def magnitudes(orient, across, piece):
        polarity, col = piece // (cols // 2), piece % (cols // 2) * 2

        def taken(k, part):
            place = ((polarity * 2 + part) * cols + col + k) * apart
            return across[pl.ds(place, window), :]

        stacked = jnp.concatenate(
            [jnp.concatenate([taken(k, 0), taken(k, 1)], axis=0) for k in range(2)], axis=1
        ).astype(jnp.bfloat16)
        found = jnp.dot(inline_ref[orient], stacked, preferred_element_type=jnp.float32)
        real_part, imag_part = found[:rows], found[rows:]
        power = real_part * real_part + imag_part * imag_part + eps_mag
        size = power * lax.rsqrt(power)
        for k in range(2):
            place = (col + k) * rows * (slot + 1) + 2 * orient + polarity
            features_ref[pl.ds(place, rows, stride=slot + 1), :] = size[
                :, k * samples : (k + 1) * samples
            ]

    def filtered(which, across, before, across_before):
        band = jnp.dot(traces[...], time_ref[which], preferred_element_type=jnp.float32)
        band = band.astype(jnp.bfloat16)
        done = 0
        for pair in range(window // 2):

            def piece(k, p):
                first = (pair * 2 + k) * lines
                return band[first : first + lines, p * samples : (p + 1) * samples]

            stacked = jnp.concatenate(
                [jnp.concatenate([piece(k, 0), piece(k, 1)], axis=0) for k in range(2)], axis=1
            )
            crossed = jnp.dot(xline_ref[which], stacked, preferred_element_type=jnp.float32)
            for k in range(2):
                across[pl.ds(2 * pair + k, 4 * cols, stride=apart), :] = crossed[
                    :, k * samples : (k + 1) * samples
                ]
            until = cols * (pair + 1) // (window // 2)
            for other in range(done, until):
                magnitudes(before, across_before, other)
            done = until

    filtered(0, across_even, jnp.maximum(2 * twice - 1, 0), across_odd)
    filtered(1, across_odd, 2 * twice, across_even)

    @pl.when(twice == orients // 2 - 1)
    def _():
        for piece in range(cols):
            magnitudes(orients - 1, across_odd, piece)

    @pl.when(twice == orients // 2 - 1)
    def _():
        matrix = score_matrix(
            params_ref[:components],
            params_ref[components : 2 * components],
            jnp.log(params_ref[2 * components :, :1]),
            feats, slot, 3,
        )
        total[...] = jnp.zeros(total.shape, jnp.float32)


        def sweep(block, moments, scoring):
            partial = jnp.zeros(total.shape, jnp.float32)
            for start in range(0, unit * cols, chunk):
                place = slice(start * samples, (start + chunk) * samples)
                if moments:
                    partial = partial + moment_stage(data[:, place], scores, place)[1]
                if scoring:
                    row = block * unit + start // cols
                    lines = gathered(features_ref, row, rows, start % cols, chunk, slot)
                    pieces = split_features(lines)
                    data[:, place] = pieces[: data.shape[0]]
                    split_ref[block, :, place] = pieces
                    score_stage(pieces, matrix, scores, place, components)
            if moments:
                total[...] += partial

        sweep(0, False, True)

        @pl.loop(1, rows // unit)
        def _(block):
            sweep(block, True, True)

        sweep(0, True, False)
        sums_ref[...] = fold_sums(total[...], components, slot)


def new_params(sums, centers, spreads, feats, slot, cells):
    components = centers.shape[0]
    mass = sums[:, feats : feats + 1]
    first = sums
    second = pltpu.roll(sums, LANES - slot, 1)
    scale = 1.0 / (mass + 1.0)
    moved = (first + centers) * scale
    centred = second - 2.0 * moved * first + moved * moved * mass
    return moved, (centred + spreads) * scale, (mass + 1.0) / (cells + components)


def posterior_kernel(dims, *refs):
    orients, samples, cols, rows, components, chunk, unit, cells = dims
    split_ref, params_ref, before_ref = refs[:3]
    posterior_ref, sums_ref, centers_ref, spreads_ref, matrix, total, turned, scores = refs[3:]
    feats = 2 * orients
    slot = round_up(feats + 2, SUBLANES)
    step = pl.program_id(0)

    @pl.when(step == 0)
    def _():
        centers, spreads, weights = new_params(
            before_ref[...],
            params_ref[:components],
            params_ref[components : 2 * components],
            feats, slot, cells,
        )
        lanes = lax.broadcasted_iota(jnp.int32, centers.shape, 1)
        centers = jnp.where(lanes < feats, centers, 0.0)
        spreads = jnp.where(lanes < feats, spreads, 1.0)
        centers_ref[...] = centers
        spreads_ref[...] = spreads
        matrix[...] = score_matrix(centers, spreads, jnp.log(weights), feats, slot, 2)
        total[...] = jnp.zeros(total.shape, jnp.float32)

    def sweep(moments, scoring):
        partial = jnp.zeros(total.shape, jnp.float32)
        for start in range(0, unit * cols, chunk):
            place = slice(start * samples, (start + chunk) * samples)
            which, col = start // cols, start % cols
            if moments:
                before = split_ref[step - 1, : 4 * slot, place]
                shares, sums = moment_stage(before, scores, place)
            if scoring:
                score_stage(split_ref[step, :, place], matrix[...], scores, place, components)
            if moments:
                partial = partial + sums
                for k in range(chunk):
                    turned[which, pl.ds(col + k, components, stride=cols + 1), :] = shares[
                        :, k * samples : (k + 1) * samples
                    ]
        if moments:
            total[...] += partial
            for which in range(unit):
                for component in range(components):
                    posterior_ref[which, component] = turned[
                        which, pl.ds(component * (cols + 1), cols), :
                    ].astype(jnp.bfloat16)

    last = rows // unit
    pl.when(step == 0)(lambda: sweep(False, True))
    pl.when((step > 0) & (step < last))(lambda: sweep(True, True))
    pl.when(step == last)(lambda: sweep(True, False))

    @pl.when(step == pl.num_programs(0) - 1)
    def _():
        sums_ref[...] = fold_sums(total[...], components, slot)


def update_kernel(dims, sums_ref, centers_ref, spreads_ref, means_ref, variances_ref, weights_ref):
    feats, slot, cells = dims
    components = sums_ref.shape[0]
    rest = jnp.zeros((LANES - 3 * components, LANES), jnp.float32)
    turned = jnp.concatenate(
        [sums_ref[...], centers_ref[...], spreads_ref[...], rest], axis=0
    ).T
    part = lambda first, group: turned[
        first : first + feats, group * components : (group + 1) * components
    ]
    mass = turned[feats : feats + 1, :components]
    first, second, centers, spreads = part(0, 0), part(slot, 0), part(0, 1), part(0, 2)
    moved = (first + centers) / (mass + 1.0)
    centred = second - 2.0 * moved * first + moved * moved * mass
    means_ref[...] = moved
    variances_ref[...] = (centred + spreads) / (mass + 1.0)
    weights_ref[...] = (mass + 1.0) / (cells + components)


def exchange(values, axis, pairs):
    return lax.ppermute(values, axis, [p for a, b in pairs for p in ((a, b), (b, a))])


def group_sum(values):
    axes = ("inline", "xline")
    count = lax.axis_size("inline") * lax.axis_size("xline")
    if count & (count - 1):
        return lax.psum(values, axes)
    rounds = []
    while count > 1:
        rounds.append(min(4, count))
        count //= rounds[-1]
    for radix in rounds:
        count *= radix
    step = count
    for radix in rounds:
        step //= radix
        arrived = [
            lax.ppermute(values, axes, [(i, i ^ (step * d)) for i in range(count)])
            for d in range(1, radix)
        ]
        if radix == 4:
            values = (values + arrived[0]) + (arrived[1] + arrived[2])
        else:
            values = values + arrived[0]
    return values


def per_device(traces, directions, init_means, init_variances, init_weights):
    rows, cols, samples = traces.shape
    orients = directions.shape[0]
    components = init_weights.shape[0]
    feats = 2 * orients
    slot = round_up(feats + 2, SUBLANES)
    window = round_up(rows + 2 * HALF, 16)
    inlines = lax.axis_size("inline")
    if lax.axis_size("xline") != 2 or samples != LANES or rows < HALF or orients % 2 or cols % 2:
        raise ValueError("unsupported sizes")

    core_pairs = [(0, 1)]
    other = exchange(traces, "xline", core_pairs)
    swap_one = exchange(traces, "inline", [(i, i + 1) for i in range(0, inlines - 1, 2)])
    swap_two = exchange(traces, "inline", [(i, i + 1) for i in range(1, inlines - 1, 2)])
    vmem = pl.BlockSpec(memory_space=pltpu.VMEM)
    time_mats, xline_mats, inline_mats, own = pl.pallas_call(
        functools.partial(matrices_kernel, (orients, samples, cols, rows, window)),
        out_shape=(
            jax.ShapeDtypeStruct((orients, samples, 2 * samples), jnp.bfloat16),
            jax.ShapeDtypeStruct((orients, 4 * cols, 4 * cols), jnp.bfloat16),
            jax.ShapeDtypeStruct((orients, 2 * rows, 2 * window), jnp.bfloat16),
            jax.ShapeDtypeStruct(traces.shape, traces.dtype),
        ),
        in_specs=[pl.BlockSpec(memory_space=pltpu.SMEM), vmem],
        out_specs=(vmem, vmem, vmem, vmem),
        compiler_params=pltpu.CompilerParams(vmem_limit_bytes=8 * 2**20),
        name="filter_matrices",
        cost_estimate=pl.CostEstimate(flops=0, bytes_accessed=4_000_000, transcendentals=0),
    )(directions, traces)

    swap_one, swap_two, time_mats, xline_mats, inline_mats, own = lax.optimization_barrier(
        (swap_one, swap_two, time_mats, xline_mats, inline_mats, own)
    )
    swap_one_other = exchange(swap_one, "xline", core_pairs)
    swap_two_other = exchange(swap_two, "xline", core_pairs)

    spread_out = lambda values, fill: jnp.pad(
        values, ((0, 0), (0, LANES - values.shape[1])), constant_values=fill
    )
    params = jnp.concatenate(
        [
            spread_out(init_means, 0.0),
            spread_out(init_variances, 1.0),
            jnp.broadcast_to(init_weights[:, None], (components, LANES)),
        ],
        axis=0,
    )
    whole = lambda *shape: pl.BlockSpec(shape, lambda o: (0,) * len(shape))
    chunk = 6
    unit = next(count for count in (8, 4, 2, 1) if rows % count == 0)
    split_shape = (rows // unit, 6 * slot, unit * cols * samples)
    pieces, sums = pl.pallas_call(
        functools.partial(
            features_kernel, (orients, samples, cols, rows, window, components, chunk, unit)
        ),
        grid=(orients // 2,),
        out_shape=(
            jax.ShapeDtypeStruct(split_shape, jnp.bfloat16),
            jax.ShapeDtypeStruct((components, LANES), jnp.float32),
        ),
        in_specs=[whole(rows, cols, samples)] * 6
        + [
            pl.BlockSpec((2, samples, 2 * samples), lambda o: (o, 0, 0)),
            pl.BlockSpec((2, 4 * cols, 4 * cols), lambda o: (o, 0, 0)),
            whole(orients, 2 * rows, 2 * window),
            whole(3 * components, LANES),
        ],
        out_specs=(whole(*split_shape), whole(components, LANES)),
        scratch_shapes=[
            pltpu.VMEM((rows * cols * (slot + 1), samples), jnp.float32),
            pltpu.VMEM((window * 2 * cols, samples), jnp.bfloat16),
            pltpu.VMEM((4 * cols * (window + 1), samples), jnp.float32),
            pltpu.VMEM((4 * cols * (window + 1), samples), jnp.float32),
            pltpu.VMEM((4 * slot, 2 * components), jnp.float32),
            pltpu.VMEM((4 * slot, unit * cols * samples), jnp.bfloat16),
            pltpu.VMEM((components, unit * cols * samples), jnp.float32),
        ],
        compiler_params=pltpu.CompilerParams(vmem_limit_bytes=28 * 2**20),
        name="features_and_first_moments",
    )(
        own, other, swap_one, swap_one_other, swap_two, swap_two_other,
        time_mats, xline_mats, inline_mats,
        params,
    )
    sums = group_sum(sums)
    cells = inlines * rows * lax.axis_size("xline") * cols * samples
    posterior, sums, centers, spreads = pl.pallas_call(
        functools.partial(
            posterior_kernel, (orients, samples, cols, rows, components, chunk, unit, cells)
        ),
        grid=(rows // unit + 1,),
        out_shape=(
            jax.ShapeDtypeStruct((rows, components, cols, samples), jnp.bfloat16),
            jax.ShapeDtypeStruct((components, LANES), jnp.float32),
            jax.ShapeDtypeStruct((components, LANES), jnp.float32),
            jax.ShapeDtypeStruct((components, LANES), jnp.float32),
        ),
        in_specs=[
            whole(*split_shape),
            whole(3 * components, LANES),
            whole(components, LANES),
        ],
        out_specs=(
            pl.BlockSpec((unit, components, cols, samples), lambda r: (jnp.maximum(r - 1, 0), 0, 0, 0)),
            whole(components, LANES),
            whole(components, LANES),
            whole(components, LANES),
        ),
        scratch_shapes=[
            pltpu.VMEM((2 * components, 6 * slot), jnp.bfloat16),
            pltpu.VMEM((4 * slot, 2 * components), jnp.float32),
            pltpu.VMEM((unit, components * (cols + 1), samples), jnp.float32),
            pltpu.VMEM((components, unit * cols * samples), jnp.float32),
        ],
        compiler_params=pltpu.CompilerParams(vmem_limit_bytes=28 * 2**20),
        name="posterior_and_second_moments",
    )(pieces, params, sums)
    sums = group_sum(sums)
    means, variances, weights = pl.pallas_call(
        functools.partial(update_kernel, (feats, slot, cells)),
        out_shape=(
            jax.ShapeDtypeStruct((feats, components), jnp.float32),
            jax.ShapeDtypeStruct((feats, components), jnp.float32),
            jax.ShapeDtypeStruct((1, components), jnp.float32),
        ),
        in_specs=[vmem, vmem, vmem],
        out_specs=(vmem, vmem, vmem),
        compiler_params=pltpu.CompilerParams(vmem_limit_bytes=8 * 2**20),
        name="last_update",
    )(sums, centers, spreads)
    return posterior, means.T, variances.T, weights.reshape(components)


def solution(mesh):
    in_specs = (P(("slab", "inline"), "xline", None), P(), P(), P(), P())
    out_specs = (
        P(("slab", "inline"), None, "xline", None),
        P("slab", None),
        P("slab", None),
        P("slab"),
    )
    return jax.shard_map(
        per_device, mesh=mesh, in_specs=in_specs, out_specs=out_specs, check_vma=False
    )
```
